512 devices in a mesh: ctx: 16 (over y, core), nbr: 8 (over z), tp: 4 (over x).
Axes of the slice: x: 4, y: 8, z: 8, core: 2. Of those that a mesh axis runs over, the one named last changes fastest.
Arguments:
- hidden: bfloat16 [32768, 4096], P(('ctx', 'nbr'), 'tp'), may hold values from -6 to 6
- queries: bfloat16 [32768, 2048], P(('ctx', 'nbr'), 'tp'), may hold values from -6 to 6
- key_weight_matrix: bfloat16 [768, 2048], P('ctx', 'tp'), may hold values from -0.21875 to 0.21875
- value_weight_matrix: bfloat16 [768, 2048], P('ctx', 'tp'), may hold values from -0.21875 to 0.21875
- w_out: bfloat16 [2048, 4096], P('ctx', 'tp'), may hold values from -0.125 to 0.125
- neighbour_embed: bfloat16 [1024, 128, 768], P(('ctx', 'nbr')), may hold values from -6 to 6
- neighbour_ids: int32 [1024, 128], P(('ctx', 'nbr')), may hold values from 0 to 127999, as said below
- neighbour_count: int32 [512], P(('ctx', 'nbr')), may hold values from 0 to 2, as said below
- slot_seq: int32 [128, 8], replicated, may hold values from 0 to 7, as said below
- cond_keys: bfloat16 [32768, 768], P(('ctx', 'nbr'), 'tp'), may hold values from -6 to 6
- cond_values: bfloat16 [32768, 768], P(('ctx', 'nbr'), 'tp'), may hold values from -6 to 6
- enc_gain: bfloat16 [768], replicated, may hold values from 0.5 to 1.5
- enc_query: bfloat16 [768, 768], P(None, 'tp'), may hold values from -0.21875 to 0.21875
- enc_out: bfloat16 [768, 768], P('tp'), may hold values from -0.21875 to 0.21875
- final_gain: bfloat16 [768], replicated, may hold values from 0.5 to 1.5
Outputs:
- output: bfloat16 [32768, 4096], P(('ctx', 'nbr'), 'tp')
The draws below stay inside these ranges and needn't reach their ends.
Inputs may be any that keep to these rules, and one draw needn't show every extreme that they name: `neighbour_ids`: every neighbour's ids are nonzero up to a length of at least 32 tokens and 0 after it. `slot_seq`: each row is a permutation of 0 to 7. `neighbour_count`: the last stretch of every block of positions has at least one valid neighbour.
All inputs are finite; a program needn't handle non-finite values.
Results may differ from the reference program's by a relative error of at most 0.0075.
Values may be sent and summed in bfloat16 or wider, within the bound.
A program may use at most 64 MiB of HBM per device.

```python
import jax
import jax.numpy as jnp
from jax import lax

DECODER_WIDTH = 4096
CROSS_HEADS = 16
HEAD_WIDTH = 128
ENCODER_WIDTH = 768
ENC_HEADS = 12
EHD = 64
VOCAB = 128000
STRETCH_TOKENS = 64
NEIGHBOUR_TOKENS = 128
NEIGHBOUR_COUNT = 2
SPO = 1
SEQS_PER_BLOCK = 8
BLOCK_STRETCHES = 4
BLOCK_TOKENS = 256
WINDOW_BLOCKS = 128
TOKENS = 32768
STRETCHES = 512
NEIGH = 1024
N_NBR = 8


def permute_row(subkey):
    return jax.random.permutation(subkey, SEQS_PER_BLOCK)


def draw_slot_seq(key, part):
    row_keys = jax.random.split(key, WINDOW_BLOCKS)
    return jax.vmap(permute_row)(row_keys).astype(jnp.int32)


def draw_neighbour_ids(key, part):
    key_len, key_val = jax.random.split(key)
    lengths = jax.random.randint(key_len, (NEIGH, 1), NEIGHBOUR_TOKENS // 4, NEIGHBOUR_TOKENS + 1)
    cross_values = jax.random.randint(key_val, (NEIGH, NEIGHBOUR_TOKENS), 1, VOCAB)
    cross_values = cross_values.at[0, 0].set(VOCAB - 1)
    position = jnp.arange(NEIGHBOUR_TOKENS, dtype=jnp.int32)[None, :]
    return jnp.where(position < lengths, cross_values, 0).astype(jnp.int32)


def draw_neighbour_count(key, part):
    key_any, key_last = jax.random.split(jax.random.fold_in(key, 7))
    anyone = jax.random.randint(key_any, (STRETCHES,), 0, NEIGHBOUR_COUNT + 1)
    lasting = jax.random.randint(key_last, (STRETCHES,), 1, NEIGHBOUR_COUNT + 1)
    position = jnp.arange(STRETCHES, dtype=jnp.int32)
    closing = position % BLOCK_STRETCHES == BLOCK_STRETCHES - 1
    counts = jnp.where(closing, lasting, anyone)
    counts = counts.at[0].set(NEIGHBOUR_COUNT)
    return counts.astype(jnp.int32)


def shard_levels(key, extent, shards, least, largest):
    def one(axis_at, blocks):
        draws = jax.random.uniform(jax.random.fold_in(jax.random.fold_in(key, 6), axis_at), (blocks,), jnp.float32, least / len(shards), largest / len(shards))
        return jnp.repeat(jnp.exp(draws), extent[axis_at] // blocks).reshape((-1,) + (1,) * (len(extent) - axis_at - 1))

    factor_of = one(*shards[0])
    for cut in shards[1:]:
        factor_of = factor_of * one(*cut)
    return factor_of


def scatter_about(own_key, shape, spread, most, cuts=(), held_as=jnp.bfloat16):
    level = shard_levels(own_key, shape, cuts, -0.22, 0.18) if cuts else 1.0
    entries = jax.random.normal(own_key, shape, jnp.float32) * spread * level
    return jnp.minimum(jnp.maximum(entries, -most), most).astype(held_as)


def setup_inputs(seed: int = 0) -> dict:
    splits = jax.random.split(jax.random.key(seed), 16)
    return {
        "hidden": scatter_about(splits[0], (TOKENS, DECODER_WIDTH), 1.0, 6.0, ((0, 128), (1, 4))),
        "queries": scatter_about(splits[1], (TOKENS, CROSS_HEADS * HEAD_WIDTH), 1.0, 6.0, ((0, 128), (1, 4))),
        "key_weight_matrix": scatter_about(splits[2], (ENCODER_WIDTH, CROSS_HEADS * HEAD_WIDTH), ENCODER_WIDTH ** -0.5, 0.21875, ((0, 16), (1, 4))),
        "value_weight_matrix": scatter_about(splits[3], (ENCODER_WIDTH, CROSS_HEADS * HEAD_WIDTH), ENCODER_WIDTH ** -0.5, 0.21875, ((0, 16), (1, 4))),
        "w_out": scatter_about(splits[4], (CROSS_HEADS * HEAD_WIDTH, DECODER_WIDTH), (CROSS_HEADS * HEAD_WIDTH) ** -0.5, 0.125, ((0, 16), (1, 4))),
        "neighbour_embed": scatter_about(splits[5], (NEIGH, NEIGHBOUR_TOKENS, ENCODER_WIDTH), 1.0, 6.0, ((0, 128),)),
        "neighbour_ids": draw_neighbour_ids(jax.random.fold_in(splits[15], 71), 0),
        "neighbour_count": draw_neighbour_count(jax.random.fold_in(splits[15], 71), 0),
        "slot_seq": draw_slot_seq(jax.random.fold_in(splits[15], 71), 0),
        "cond_keys": scatter_about(splits[9], (TOKENS, ENCODER_WIDTH), 1.0, 6.0, ((0, 128), (1, 4))),
        "cond_values": scatter_about(splits[10], (TOKENS, ENCODER_WIDTH), 1.0, 6.0, ((0, 128), (1, 4))),
        "enc_gain": jnp.clip(1.0 + 0.1 * jax.random.normal(splits[11], (ENCODER_WIDTH,), jnp.float32), 0.5, 1.5).astype(jnp.bfloat16),
        "enc_query": scatter_about(splits[12], (ENCODER_WIDTH, ENCODER_WIDTH), ENCODER_WIDTH ** -0.5, 0.21875, ((1, 4),)),
        "enc_out": scatter_about(splits[13], (ENCODER_WIDTH, ENCODER_WIDTH), ENCODER_WIDTH ** -0.5, 0.21875, ((0, 4),)),
        "final_gain": jnp.clip(1.0 + 0.1 * jax.random.normal(splits[14], (ENCODER_WIDTH,), jnp.float32), 0.5, 1.5).astype(jnp.bfloat16),
    }


EPSILON = 1e-06

def row_rscale(matrix):
    return lax.rsqrt(lax.optimization_barrier(jnp.mean(matrix * matrix, axis=-1, keepdims=True)) + EPSILON)

def masked_attend(query_rows, key_rows, value_rows, allowed, score_scale):
    scores = jnp.einsum('bqhd,bkhd->bhqk', query_rows.astype(jnp.float32), key_rows.astype(jnp.float32)) * score_scale
    allowed_map = allowed[:, None, None, :]
    highest = lax.optimization_barrier(jnp.max(jnp.where(allowed_map, scores, -1e+30), axis=-1, keepdims=True))
    raised = jnp.where(allowed_map, jnp.exp(scores - highest), 0.0)
    totals = lax.optimization_barrier(jnp.sum(raised, axis=-1, keepdims=True))
    anyone = jnp.any(allowed, axis=-1)[:, None, None, None]
    weights = (raised / jnp.where(anyone, totals, 1.0)).astype(jnp.bfloat16)
    return jnp.einsum('bhqk,bkhd->bqhd', weights.astype(jnp.float32), value_rows.astype(jnp.float32)).astype(jnp.bfloat16)

def reference(hidden, queries, key_weight_matrix, value_weight_matrix, w_out, neighbour_embed, neighbour_ids, neighbour_count, slot_seq, cond_keys, cond_values, enc_gain, enc_query, enc_out, final_gain):
    row_index = jnp.arange(NEIGH, dtype=jnp.int32)
    slot_pos = row_index % SPO
    block_in_group = row_index // SPO % N_NBR
    owner = row_index // SEQS_PER_BLOCK % N_NBR
    group = row_index // (SEQS_PER_BLOCK * N_NBR)
    current_block = (group * N_NBR + block_in_group).astype(jnp.int32)
    sequence_in_block = slot_seq[current_block, owner * SPO + slot_pos].astype(jnp.int32)
    stretch_lookup = (current_block * BLOCK_STRETCHES + sequence_in_block // NEIGHBOUR_COUNT).astype(jnp.int32)
    dest = (current_block * SEQS_PER_BLOCK + sequence_in_block).astype(jnp.int32)
    key_rows = jnp.take(cond_keys.reshape(STRETCHES, STRETCH_TOKENS, ENCODER_WIDTH), stretch_lookup, axis=0).reshape(WINDOW_BLOCKS, SEQS_PER_BLOCK, STRETCH_TOKENS, ENCODER_WIDTH)
    value_rows = jnp.take(cond_values.reshape(STRETCHES, STRETCH_TOKENS, ENCODER_WIDTH), stretch_lookup, axis=0).reshape(WINDOW_BLOCKS, SEQS_PER_BLOCK, STRETCH_TOKENS, ENCODER_WIDTH)

    def encode_block(stretch_parts):
        embed_rows, keys_here, values_here = stretch_parts
        wide = embed_rows.astype(jnp.float32).reshape(SEQS_PER_BLOCK * NEIGHBOUR_TOKENS, ENCODER_WIDTH)
        normed = (wide * row_rscale(wide) * enc_gain.astype(jnp.float32)).astype(jnp.bfloat16)
        enc_q = jnp.dot(normed, enc_query, preferred_element_type=jnp.float32).astype(jnp.bfloat16)
        enc_q = enc_q.reshape(SEQS_PER_BLOCK, NEIGHBOUR_TOKENS, ENC_HEADS, EHD)
        mixed = masked_attend(enc_q, keys_here.reshape(SEQS_PER_BLOCK, STRETCH_TOKENS, ENC_HEADS, EHD), values_here.reshape(SEQS_PER_BLOCK, STRETCH_TOKENS, ENC_HEADS, EHD), jnp.ones((SEQS_PER_BLOCK, STRETCH_TOKENS), dtype=bool), EHD ** (-0.5))
        updated = wide + jnp.dot(mixed.reshape(SEQS_PER_BLOCK * NEIGHBOUR_TOKENS, ENCODER_WIDTH), enc_out, preferred_element_type=jnp.float32)
        return (updated * row_rscale(updated) * final_gain.astype(jnp.float32)).astype(jnp.bfloat16).reshape(SEQS_PER_BLOCK, NEIGHBOUR_TOKENS, ENCODER_WIDTH)
    encoded = lax.map(encode_block, (neighbour_embed.reshape(WINDOW_BLOCKS, SEQS_PER_BLOCK, NEIGHBOUR_TOKENS, ENCODER_WIDTH), key_rows, value_rows)).reshape(NEIGH, NEIGHBOUR_TOKENS, ENCODER_WIDTH)
    ordered_encoded_rows = jnp.zeros_like(encoded).at[dest].set(encoded)
    valid_entries = (jnp.arange(NEIGHBOUR_COUNT, dtype=jnp.int32)[None, :, None] < neighbour_count[:, None, None]) & (neighbour_ids.reshape(STRETCHES, NEIGHBOUR_COUNT, NEIGHBOUR_TOKENS) != 0)
    valid_entries = valid_entries.reshape(WINDOW_BLOCKS, BLOCK_STRETCHES, NEIGHBOUR_COUNT * NEIGHBOUR_TOKENS)

    def one_block(carry, stretch_parts):
        prev_keys, prev_values, prev_valid = carry
        enc_rows, valid_rows, query_rows, hidden_rows = stretch_parts
        flattened_rows = enc_rows.reshape(SEQS_PER_BLOCK * NEIGHBOUR_TOKENS, ENCODER_WIDTH)
        cross_keys = jnp.dot(flattened_rows, key_weight_matrix, preferred_element_type=jnp.float32).astype(jnp.bfloat16).reshape(BLOCK_STRETCHES, NEIGHBOUR_COUNT * NEIGHBOUR_TOKENS, CROSS_HEADS, HEAD_WIDTH)
        cross_values = jnp.dot(flattened_rows, value_weight_matrix, preferred_element_type=jnp.float32).astype(jnp.bfloat16).reshape(BLOCK_STRETCHES, NEIGHBOUR_COUNT * NEIGHBOUR_TOKENS, CROSS_HEADS, HEAD_WIDTH)
        then_keys = jnp.concatenate([prev_keys[None], cross_keys[:-1]], axis=0)
        then_values = jnp.concatenate([prev_values[None], cross_values[:-1]], axis=0)
        then_valid = jnp.concatenate([prev_valid[None], valid_rows[:-1]], axis=0)
        early = masked_attend(query_rows[:, :STRETCH_TOKENS - 1], then_keys, then_values, then_valid, HEAD_WIDTH ** (-0.5))
        last = masked_attend(query_rows[:, STRETCH_TOKENS - 1:], cross_keys, cross_values, valid_rows, HEAD_WIDTH ** (-0.5))
        attended = jnp.concatenate([early, last], axis=1).reshape(BLOCK_TOKENS, CROSS_HEADS * HEAD_WIDTH)
        result = (hidden_rows.astype(jnp.float32) + jnp.dot(attended, w_out, preferred_element_type=jnp.float32)).astype(jnp.bfloat16)
        return ((cross_keys[-1], cross_values[-1], valid_rows[-1]), result)
    start = (jnp.zeros((NEIGHBOUR_COUNT * NEIGHBOUR_TOKENS, CROSS_HEADS, HEAD_WIDTH), jnp.bfloat16), jnp.zeros((NEIGHBOUR_COUNT * NEIGHBOUR_TOKENS, CROSS_HEADS, HEAD_WIDTH), jnp.bfloat16), jnp.zeros((NEIGHBOUR_COUNT * NEIGHBOUR_TOKENS,), dtype=bool))
    stretch_parts = (ordered_encoded_rows.reshape(WINDOW_BLOCKS, SEQS_PER_BLOCK, NEIGHBOUR_TOKENS, ENCODER_WIDTH), valid_entries, queries.reshape(WINDOW_BLOCKS, BLOCK_STRETCHES, STRETCH_TOKENS, CROSS_HEADS, HEAD_WIDTH), hidden.reshape(WINDOW_BLOCKS, BLOCK_TOKENS, DECODER_WIDTH))
    unused, results = lax.scan(one_block, start, stretch_parts)
    return results.reshape(TOKENS, DECODER_WIDTH)
```

```python
import jax
import jax.numpy as jnp
from jax import lax
from jax.experimental import pallas as pl
from jax.experimental.pallas import tpu as pltpu
from jax.sharding import PartitionSpec as P

HEAD_WIDTH = 128
EHD = 64
STRETCH_TOKENS = 64
NEIGHBOUR_TOKENS = 128
EPSILON = 1e-06
MESH = pl.DeviceIdType.MESH
NT = (((1,), (1,)), ((), ()))
TN = (((0,), (0,)), ((), ()))
NN = (((1,), (0,)), ((), ()))

S_EMB, S_COND, S_ENC_W, S_KV_RIGHT, S_KV_LEFT, S_KV_MATE, S_MASK, S_AG, S_PREV, S_ATT = (
    0, 2, 5, 13, 17, 20, 21, 22, 28, 29,
)
N_SEMS = 35


def dot(a, b, dims):
    return lax.dot_general(a, b, dims, preferred_element_type=jnp.float32)


def norm_rows(rows, gain):
    scale = lax.rsqrt(jnp.mean(rows * rows, axis=-1, keepdims=True) + EPSILON)
    return (rows * scale * gain).astype(jnp.bfloat16)


def body(
    slots, counts, embed, cond_k_far, cond_v_far, enc_q, enc_o, key_w, value_w, queries_far, ids_far, gain_in, gain_out,
    attended,
    cond_k, cond_v, queries, ids,
    emb, packs, cond_send, cond, enc_w, normed, mixed, encoded, kv_w, keys, values,
    last_send, last_got, mask_send, mask_got, key_mask, partial, send, recv, local,
):
    c, n, t = lax.axis_index("ctx"), lax.axis_index("nbr"), lax.axis_index("tp")
    block = c * 8 + n
    right, left, across = lax.rem(t + 1, 4), lax.rem(t + 3, 4), lax.rem(t + 2, 4)
    core = lax.rem(c, 2)
    y = c // 2
    mate = c + 1 - 2 * core
    c_right, c_left = lax.rem(c + 2, 16), lax.rem(c + 14, 16)
    first = lax.rem(t - n + 8, 4)
    nxt = lax.rem(block + 1, 128)
    before = lax.rem(block + 127, 128)
    next_device = (nxt // 8, lax.rem(nxt, 8), t)
    before_device = (before // 8, lax.rem(before, 8), t)

    def copy(src, dst, s, r, device):
        return pltpu.make_async_remote_copy(
            src_ref=src, dst_ref=dst, send_sem=send.at[s], recv_sem=recv.at[r],
            device_id=device, device_id_type=MESH,
        )

    def to(ref, s, device, dst=None, r=None):
        made = copy(ref, ref if dst is None else dst, s, s if r is None else r, device)
        made.start()
        sent.append(made)

    def arrived(ref, r):
        copy(ref, ref, r, r, (c, n, right)).wait_recv()

    sent = []

    own = [
        pltpu.make_async_copy(enc_q, enc_w.at[0, t], local.at[0]),
        pltpu.make_async_copy(enc_o, enc_w.at[1, t], local.at[1]),
        pltpu.make_async_copy(key_w, kv_w.at[0, y, core], local.at[2]),
        pltpu.make_async_copy(value_w, kv_w.at[1, y, core], local.at[3]),
        pltpu.make_async_copy(cond_k_far, cond_k, local.at[5]),
        pltpu.make_async_copy(cond_v_far, cond_v, local.at[6]),
        pltpu.make_async_copy(queries_far, queries, local.at[7]),
        pltpu.make_async_copy(ids_far, ids, local.at[8]),
    ]
    for made in own:
        made.start()

    barrier = pltpu.get_barrier_semaphore()
    for device in (
        (c, n, right), (c, n, left), (c, n, across), (mate, n, t), (c_right, n, t), (c_left, n, t), before_device,
    ):
        pl.semaphore_signal(barrier, inc=1, device_id=device, device_id_type=MESH)
    for k in range(2):
        other = first + 4 * k

        @pl.when(other != n)
        def _():
            pl.semaphore_signal(barrier, inc=1, device_id=(c, other, t), device_id_type=MESH)

    with_self = jnp.where(lax.rem(2 * n, 4) == t, 1, 0)
    pl.semaphore_wait(barrier, 9 - with_self)

    mine = n // 4

    def emb_copy(k):
        other = first + 4 * k
        return copy(embed.at[other], emb.at[mine], S_EMB + k, S_EMB + mine, (c, other, t))

    for k in range(2):
        other = first + 4 * k

        @pl.when(other != n)
        def _():
            emb_copy(k).start()

        @pl.when(other == n)
        def _():
            pltpu.make_async_copy(embed.at[n], emb.at[mine], local.at[4]).start()

    own[0].wait()
    own[1].wait()
    to(enc_w.at[:, t, core], S_ENC_W, (c, n, right))
    to(enc_w.at[:, t, core], S_ENC_W + 1, (c, n, left))

    own[4].wait()
    own[5].wait()
    for st in range(4):
        at = slice(st * STRETCH_TOKENS, (st + 1) * STRETCH_TOKENS)
        packs[st] = jnp.concatenate([cond_k[:, at], cond_v[:, at]], axis=1)
    for d in (1, 3, 2):
        target = lax.rem(t + d, 4)
        start = lax.rem(target - n + 8, 4)
        for k in range(2):
            cond_send[d - 1, k] = packs[slots[start + 4 * k, block] // 2]
        to(cond_send.at[d - 1], S_COND + d - 1, (c, n, target), dst=cond.at[t])
    for k in range(2):
        cond[t, k] = packs[slots[first + 4 * k, block] // 2]

    own[2].wait()
    own[3].wait()

    def kv_right(s):
        to(kv_w.at[:, lax.rem(y - s + 8, 8), core], S_KV_RIGHT + s, (c_right, n, t))

    def kv_left(s):
        to(kv_w.at[:, lax.rem(y + s, 8), core], S_KV_LEFT + s, (c_left, n, t))

    def kv_right_in(s):
        arrived(kv_w.at[:, lax.rem(y - s - 1 + 8, 8), core], S_KV_RIGHT + s)

    def kv_left_in(s):
        arrived(kv_w.at[:, lax.rem(y + s + 1, 8), core], S_KV_LEFT + s)

    kv_right(0)
    kv_left(0)

    own[7].wait()
    row = lax.broadcasted_iota(jnp.int32, (8, 128), 0)
    count = jnp.zeros((8, 128), jnp.int32)
    for st in range(4):
        count = jnp.where(row // 2 == st, counts[st], count)
    mask_send[...] = jnp.where((lax.rem(row, 2) < count) & (ids[...] != 0), 1.0, 0.0)
    to(mask_send, S_MASK, next_device, dst=mask_got)
    mask = mask_send[...]
    for s in range(8):
        key_mask[s] = jnp.broadcast_to(mask[s : s + 1], (128, 128)).T

    for k in range(2):
        other = first + 4 * k

        @pl.when(other != n)
        def _():
            arrived(emb.at[k], S_EMB + k)

        @pl.when(other == n)
        def _():
            pltpu.make_async_copy(embed.at[n], emb.at[k], local.at[4]).wait()

        normed[k] = norm_rows(emb[k].astype(jnp.float32), gain_in[...].astype(jnp.float32))

    def encode_heads(shard):
        query = dot(enc_w[0, shard].reshape(192, 768), normed[...].reshape(256, 768), NT)
        query = query.astype(jnp.bfloat16) * jnp.bfloat16(EHD ** (-0.5))
        columns = []
        for k in range(2):
            rows = []
            for h in range(3):
                at = slice(h * EHD, (h + 1) * EHD)
                both = cond[shard, k, at, :]
                scores = dot(both, query[at, k * 128 : (k + 1) * 128], TN)[:STRETCH_TOKENS]
                raised = jnp.exp(scores - jnp.max(scores, axis=0, keepdims=True))
                weights = (raised / jnp.sum(raised, axis=0, keepdims=True)).astype(jnp.bfloat16)
                spread = jnp.concatenate([jnp.zeros_like(weights), weights], axis=0)
                rows.append(dot(both, spread, NN).astype(jnp.bfloat16))
            columns.append(jnp.concatenate(rows, axis=0))
        mixed[shard] = jnp.concatenate(columns, axis=1)

    encode_heads(t)

    kv_right_in(0)
    kv_right(1)
    kv_left_in(0)
    kv_left(1)

    arrived(enc_w.at[:, left, core], S_ENC_W)
    to(enc_w.at[0, left, core], S_ENC_W + 2, (c, n, right))
    to(enc_w.at[:, left, core], S_ENC_W + 4, (mate, n, t))
    arrived(enc_w.at[:, right, core], S_ENC_W + 1)
    to(enc_w.at[1, right, core], S_ENC_W + 3, (c, n, left))
    to(enc_w.at[:, right, core], S_ENC_W + 5, (mate, n, t))
    arrived(cond.at[left], S_COND)
    arrived(enc_w.at[:, left, 1 - core], S_ENC_W + 4)
    encode_heads(left)
    kv_right_in(1)
    kv_right(2)
    kv_left_in(1)
    kv_left(2)
    arrived(enc_w.at[0, across, core], S_ENC_W + 2)
    to(enc_w.at[0, across, core], S_ENC_W + 6, (mate, n, t))
    arrived(enc_w.at[1, across, core], S_ENC_W + 3)
    to(enc_w.at[1, across, core], S_ENC_W + 7, (mate, n, t))
    arrived(cond.at[right], S_COND + 2)
    arrived(enc_w.at[:, right, 1 - core], S_ENC_W + 5)
    encode_heads(right)
    kv_right_in(2)
    kv_right(3)
    arrived(cond.at[across], S_COND + 1)
    arrived(enc_w.at[0, across, 1 - core], S_ENC_W + 6)
    encode_heads(across)
    arrived(enc_w.at[1, across, 1 - core], S_ENC_W + 7)

    updated = dot(mixed[...].reshape(768, 256), enc_w[1].reshape(768, 768), TN)
    gain = gain_out[...].astype(jnp.float32)
    for k in range(2):
        rows = emb[k].astype(jnp.float32) + updated[k * 128 : (k + 1) * 128]
        encoded[first + 4 * k] = norm_rows(rows, gain)

    for k in range(2):
        to(encoded.at[first + 4 * k], S_AG + 2 * k, (c, n, right))
        to(encoded.at[first + 4 * k], S_AG + 2 * k + 1, (c, n, left))

    kv_left_in(2)
    kv_right_in(3)
    to(kv_w.at[:, :, core], S_KV_MATE, (mate, n, t))
    arrived(kv_w.at[:, :, 1 - core], S_KV_MATE)

    def project(rows):
        made = []
        for i in range(2):
            made.append(dot(rows, kv_w[i].reshape(768, 512), NN).astype(jnp.bfloat16))
        return made

    def project_pair(start):
        rows = jnp.concatenate([encoded[start], encoded[start + 4]], axis=0)
        got_k, got_v = project(rows)
        for k in range(2):
            keys[start + 4 * k] = got_k[k * 128 : (k + 1) * 128]
            values[start + 4 * k] = got_v[k * 128 : (k + 1) * 128]

    def first_of(shard):
        return lax.rem(shard - n + 8, 4)

    project_pair(first)
    arrived(encoded.at[first_of(left)], S_AG)
    to(encoded.at[first_of(left)], S_AG + 4, (c, n, right))
    arrived(encoded.at[first_of(right) + 4], S_AG + 3)
    to(encoded.at[first_of(right) + 4], S_AG + 5, (c, n, left))
    arrived(encoded.at[first_of(left) + 4], S_AG + 2)
    project_pair(first_of(left))
    arrived(encoded.at[first_of(right)], S_AG + 1)
    project_pair(first_of(right))
    arrived(encoded.at[first_of(across)], S_AG + 4)
    arrived(encoded.at[first_of(across) + 4], S_AG + 5)

    slot_of = []
    for s in range(8):
        place = jnp.int32(0)
        for o in range(1, 8):
            place = jnp.where(slots[o, block] == s, o, place)
        slot_of.append(place)
    for k in range(2):
        last_send[k] = encoded[slot_of[6 + k]]
    to(last_send, S_PREV, next_device, dst=last_got)
    project_pair(first_of(across))

    own[6].wait()
    lane = lax.broadcasted_iota(jnp.int32, (1, 128), 1)

    def attend(key_rows, value_rows, allowed, h, start, low, high):
        at = slice(h * HEAD_WIDTH, (h + 1) * HEAD_WIDTH)
        scores = dot(key_rows, queries[start : start + 128, at], NT) * HEAD_WIDTH ** (-0.5)
        scores = jnp.where(allowed > 0, scores, -1e30)
        raised = jnp.exp(scores - jnp.max(scores, axis=0, keepdims=True)) * allowed
        total = jnp.sum(raised, axis=0, keepdims=True)
        use = (total > 0) & (lane >= low) & (lane < high)
        share = jnp.where(use, 1.0 / jnp.where(use, total, 1.0), 0.0)
        return dot((raised * share).astype(jnp.bfloat16), value_rows, TN)

    def stretch_attend(st, h, start, low, high):
        at = slice(h * HEAD_WIDTH, (h + 1) * HEAD_WIDTH)
        pair = (slot_of[2 * st], slot_of[2 * st + 1])
        key_rows = jnp.concatenate([keys[p, :, at] for p in pair], axis=0)
        value_rows = jnp.concatenate([values[p, :, at] for p in pair], axis=0)
        allowed = key_mask[2 * st : 2 * st + 2].reshape(256, 128)
        return attend(key_rows, value_rows, allowed, h, start, low, high)

    for h in range(4):
        at = slice(h * HEAD_WIDTH, (h + 1) * HEAD_WIDTH)
        one = stretch_attend(0, h, 0, 63, 127)
        two = stretch_attend(1, h, 64, 63, 127)
        three = stretch_attend(2, h, 128, 63, 127)
        four = stretch_attend(3, h, 128, 127, 128)
        partial[:, at] = jnp.concatenate([one[:64], one[64:] + two[:64]], axis=0)
        lower = jnp.concatenate([two[64:] + three[:64] + four[:64], three[64:] + four[64:]], axis=0)
        attended[128:256, pl.ds(pl.multiple_of(t * 512 + h * 128, 128), 128)] = lower.astype(jnp.bfloat16)

    def piece(half, shard):
        return attended.at[pl.ds(128 * half, 128), pl.ds(pl.multiple_of(shard * 512, 512), 512)]

    to(piece(1, t), S_ATT, (c, n, right))
    to(piece(1, t), S_ATT + 1, (c, n, left))

    arrived(mask_got, S_MASK)
    seen = mask_got[...] * jnp.where(block > 0, 1.0, 0.0)
    allowed = jnp.concatenate(
        [jnp.broadcast_to(seen[6 + k : 7 + k], (128, 128)).T for k in range(2)], axis=0
    )
    arrived(last_got, S_PREV)
    got_k, got_v = project(last_got[...].reshape(256, 768))
    for h in range(4):
        at = slice(h * HEAD_WIDTH, (h + 1) * HEAD_WIDTH)
        upper = partial[:, at] + attend(got_k[:, at], got_v[:, at], allowed, h, 0, 0, 63)
        attended[0:128, pl.ds(pl.multiple_of(t * 512 + h * 128, 128), 128)] = upper.astype(jnp.bfloat16)

    to(piece(0, t), S_ATT + 2, (c, n, right))
    to(piece(0, t), S_ATT + 3, (c, n, left))
    arrived(piece(1, left), S_ATT)
    to(piece(1, left), S_ATT + 4, (c, n, right))
    arrived(piece(0, right), S_ATT + 3)
    to(piece(0, right), S_ATT + 5, (c, n, left))
    arrived(piece(1, right), S_ATT + 1)
    arrived(piece(0, left), S_ATT + 2)
    arrived(piece(1, across), S_ATT + 4)
    arrived(piece(0, across), S_ATT + 5)

    for k in range(2):

        @pl.when(first + 4 * k != n)
        def _():
            emb_copy(k).wait_send()

    for made in sent:
        made.wait_send()


def per_device(
    hidden,
    queries,
    key_weight_matrix,
    value_weight_matrix,
    w_out,
    neighbour_embed,
    neighbour_ids,
    neighbour_count,
    slot_seq,
    cond_keys,
    cond_values,
    enc_gain,
    enc_query,
    enc_out,
    final_gain,
):
    out_rows = lax.all_gather(w_out, "ctx", axis=0, tiled=True)
    vmem, hbm = pl.BlockSpec(memory_space=pltpu.VMEM), pl.BlockSpec(memory_space=pltpu.HBM)
    smem = pl.BlockSpec(memory_space=pltpu.SMEM)
    bf16, f32 = jnp.bfloat16, jnp.float32
    attended = pl.pallas_call(
        body,
        out_shape=jax.ShapeDtypeStruct((256, 2048), bf16),
        in_specs=[smem, smem, *[hbm] * 9, vmem, vmem],
        out_specs=vmem,
        scratch_shapes=[
            pltpu.VMEM((192, 256), bf16),
            pltpu.VMEM((192, 256), bf16),
            pltpu.VMEM((256, 512), bf16),
            pltpu.VMEM((8, 128), jnp.int32),
            pltpu.VMEM((2, 128, 768), bf16),
            pltpu.VMEM((4, 192, 128), bf16),
            pltpu.VMEM((3, 2, 192, 128), bf16),
            pltpu.VMEM((4, 2, 192, 128), bf16),
            pltpu.VMEM((2, 4, 2, 96, 768), bf16),
            pltpu.VMEM((2, 128, 768), bf16),
            pltpu.VMEM((4, 192, 256), bf16),
            pltpu.VMEM((8, 128, 768), bf16),
            pltpu.VMEM((2, 8, 2, 48, 512), bf16),
            pltpu.VMEM((8, 128, 512), bf16),
            pltpu.VMEM((8, 128, 512), bf16),
            pltpu.VMEM((2, 128, 768), bf16),
            pltpu.VMEM((2, 128, 768), bf16),
            pltpu.VMEM((8, 128), f32),
            pltpu.VMEM((8, 128), f32),
            pltpu.VMEM((8, 128, 128), f32),
            pltpu.VMEM((128, 512), f32),
            pltpu.SemaphoreType.DMA((N_SEMS,)),
            pltpu.SemaphoreType.DMA((N_SEMS,)),
            pltpu.SemaphoreType.DMA((9,)),
        ],
        compiler_params=pltpu.CompilerParams(
            collective_id=0, has_side_effects=True, vmem_limit_bytes=40 * 2**20
        ),
        cost_estimate=pl.CostEstimate(flops=4 * 10**9, bytes_accessed=150 * 10**6, transcendentals=0),
    )(
        slot_seq.T,
        neighbour_count,
        neighbour_embed,
        cond_keys.T,
        cond_values.T,
        enc_query.T.reshape(2, 96, 768),
        enc_out.reshape(2, 96, 768),
        key_weight_matrix,
        value_weight_matrix,
        queries,
        neighbour_ids,
        enc_gain.reshape(1, 768),
        final_gain.reshape(1, 768),
    )
    mixed_out = jnp.dot(attended, out_rows, preferred_element_type=jnp.float32)
    return (hidden.astype(jnp.float32) + mixed_out).astype(jnp.bfloat16)


def solution(mesh):
    in_specs = (
        P(("ctx", "nbr"), "tp"),
        P(("ctx", "nbr"), "tp"),
        P("ctx", "tp"),
        P("ctx", "tp"),
        P("ctx", "tp"),
        P(("ctx", "nbr"), None, None),
        P(("ctx", "nbr"), None),
        P(("ctx", "nbr")),
        P(),
        P(("ctx", "nbr"), "tp"),
        P(("ctx", "nbr"), "tp"),
        P(),
        P(None, "tp"),
        P("tp", None),
        P(),
    )
    out_specs = P(("ctx", "nbr"), "tp")
    return jax.shard_map(
        per_device, mesh=mesh, in_specs=in_specs, out_specs=out_specs, check_vma=False
    )
```

```python
import jax
import jax.numpy as jnp
from jax import lax
from jax.experimental import pallas as pl
from jax.experimental.pallas import tpu as pltpu
from jax.sharding import PartitionSpec as P

HEAD_WIDTH = 128
EHD = 64
STRETCH_TOKENS = 64
NEIGHBOUR_TOKENS = 128
EPSILON = 1e-06
MESH = pl.DeviceIdType.MESH
NT = (((1,), (1,)), ((), ()))
TN = (((0,), (0,)), ((), ()))
NN = (((1,), (0,)), ((), ()))

S_EMB, S_COND, S_ENC_W, S_KV_RIGHT, S_KV_LEFT, S_KV_MATE, S_QUERY, S_AG, S_PREV, S_ATT = (
    0, 2, 5, 13, 17, 20, 21, 22, 28, 29,
)
S_OUT_RIGHT, S_OUT_LEFT, S_OUT_MATE = 35, 39, 42
N_SEMS = 50


def dot(a, b, dims):
    return lax.dot_general(a, b, dims, preferred_element_type=jnp.float32)


def norm_rows(rows, gain):
    scale = lax.rsqrt(jnp.mean(rows * rows, axis=-1, keepdims=True) + EPSILON)
    return (rows * scale * gain).astype(jnp.bfloat16)


def body(
    slots, counts, embed, cond_k_far, cond_v_far, enc_q, enc_o, key_w, value_w, queries_far, ids_far, w_far, hidden_far,
    gain_in, gain_out,
    output,
    cond_k, cond_v, queries, ids, w_out, hidden, total, attended, queries_next, rows_send, rows_got,
    emb, packs, cond_send, cond, enc_w, normed, mixed, encoded, kv_w, keys, values, key_mask, send, recv, local,
):
    c, n, t = lax.axis_index("ctx"), lax.axis_index("nbr"), lax.axis_index("tp")
    block = c * 8 + n
    right, left, across = lax.rem(t + 1, 4), lax.rem(t + 3, 4), lax.rem(t + 2, 4)
    core = lax.rem(c, 2)
    y = c // 2
    mate = c + 1 - 2 * core
    c_right, c_left = lax.rem(c + 2, 16), lax.rem(c + 14, 16)
    first = lax.rem(t - n + 8, 4)
    nxt = lax.rem(block + 1, 128)
    before = lax.rem(block + 127, 128)
    next_device = (nxt // 8, lax.rem(nxt, 8), t)
    before_device = (before // 8, lax.rem(before, 8), t)

    def copy(src, dst, s, r, device):
        return pltpu.make_async_remote_copy(
            src_ref=src, dst_ref=dst, send_sem=send.at[s], recv_sem=recv.at[r],
            device_id=device, device_id_type=MESH,
        )

    def to(ref, s, device, dst=None, r=None):
        made = copy(ref, ref if dst is None else dst, s, s if r is None else r, device)
        made.start()
        sent.append(made)

    def arrived(ref, r):
        copy(ref, ref, r, r, (c, n, right)).wait_recv()

    sent = []

    own = [
        pltpu.make_async_copy(enc_q, enc_w.at[0, t], local.at[0]),
        pltpu.make_async_copy(enc_o, enc_w.at[1, t], local.at[1]),
        pltpu.make_async_copy(key_w, kv_w.at[0, y, core], local.at[2]),
        pltpu.make_async_copy(value_w, kv_w.at[1, y, core], local.at[3]),
        pltpu.make_async_copy(cond_k_far, cond_k, local.at[5]),
        pltpu.make_async_copy(cond_v_far, cond_v, local.at[6]),
        pltpu.make_async_copy(queries_far, queries, local.at[7]),
        pltpu.make_async_copy(ids_far, ids, local.at[8]),
        pltpu.make_async_copy(w_far, w_out.at[y, core], local.at[9]),
        pltpu.make_async_copy(hidden_far, hidden, local.at[10]),
    ]
    for made in own:
        made.start()

    barrier = pltpu.get_barrier_semaphore()
    for device in (
        (c, n, right), (c, n, left), (c, n, across), (mate, n, t), (c_right, n, t), (c_left, n, t), before_device,
        next_device,
    ):
        pl.semaphore_signal(barrier, inc=1, device_id=device, device_id_type=MESH)
    for k in range(2):
        other = first + 4 * k

        @pl.when(other != n)
        def _():
            pl.semaphore_signal(barrier, inc=1, device_id=(c, other, t), device_id_type=MESH)

    with_self = jnp.where(lax.rem(2 * n, 4) == t, 1, 0)
    pl.semaphore_wait(barrier, 10 - with_self)

    mine = n // 4

    def emb_copy(k):
        other = first + 4 * k
        return copy(embed.at[other], emb.at[mine], S_EMB + k, S_EMB + mine, (c, other, t))

    for k in range(2):
        other = first + 4 * k

        @pl.when(other != n)
        def _():
            emb_copy(k).start()

        @pl.when(other == n)
        def _():
            pltpu.make_async_copy(embed.at[n], emb.at[mine], local.at[4]).start()

    own[0].wait()
    own[1].wait()
    to(enc_w.at[:, t, core], S_ENC_W, (c, n, right))
    to(enc_w.at[:, t, core], S_ENC_W + 1, (c, n, left))

    own[2].wait()
    own[3].wait()

    def kv_right(s):
        to(kv_w.at[:, lax.rem(y - s + 8, 8), core], S_KV_RIGHT + s, (c_right, n, t))

    def kv_left(s):
        to(kv_w.at[:, lax.rem(y + s, 8), core], S_KV_LEFT + s, (c_left, n, t))

    def kv_right_in(s):
        arrived(kv_w.at[:, lax.rem(y - s - 1 + 8, 8), core], S_KV_RIGHT + s)

    def kv_left_in(s):
        arrived(kv_w.at[:, lax.rem(y + s + 1, 8), core], S_KV_LEFT + s)

    def out_right(s):
        to(w_out.at[lax.rem(y - s + 8, 8), core], S_OUT_RIGHT + s, (c_right, n, t))

    def out_left(s):
        to(w_out.at[lax.rem(y + s, 8), core], S_OUT_LEFT + s, (c_left, n, t))

    def out_right_in(s):
        arrived(w_out.at[lax.rem(y - s - 1 + 8, 8), core], S_OUT_RIGHT + s)
        to(w_out.at[lax.rem(y - s - 1 + 8, 8), core], S_OUT_MATE + 1 + s, (mate, n, t))

    def out_left_in(s):
        arrived(w_out.at[lax.rem(y + s + 1, 8), core], S_OUT_LEFT + s)
        to(w_out.at[lax.rem(y + s + 1, 8), core], S_OUT_MATE + 5 + s, (mate, n, t))

    kv_right(0)
    kv_left(0)

    own[4].wait()
    own[5].wait()
    for st in range(4):
        at = slice(st * STRETCH_TOKENS, (st + 1) * STRETCH_TOKENS)
        packs[st] = jnp.concatenate([cond_k[:, at], cond_v[:, at]], axis=1)
    for d in (1, 3, 2):
        target = lax.rem(t + d, 4)
        start = lax.rem(target - n + 8, 4)
        for k in range(2):
            cond_send[d - 1, k] = packs[slots[start + 4 * k, block] // 2]
        to(cond_send.at[d - 1], S_COND + d - 1, (c, n, target), dst=cond.at[t])
    for k in range(2):
        cond[t, k] = packs[slots[first + 4 * k, block] // 2]

    own[6].wait()
    to(queries.at[pl.ds(0, STRETCH_TOKENS)], S_QUERY, before_device, dst=queries_next)
    own[8].wait()
    out_right(0)
    out_left(0)
    to(w_out.at[y, core], S_OUT_MATE, (mate, n, t))

    own[7].wait()
    row = lax.broadcasted_iota(jnp.int32, (8, 128), 0)
    count = jnp.zeros((8, 128), jnp.int32)
    for st in range(4):
        count = jnp.where(row // 2 == st, counts[st], count)
    mask = jnp.where((lax.rem(row, 2) < count) & (ids[...] != 0), 1.0, 0.0)
    for s in range(8):
        key_mask[s] = jnp.broadcast_to(mask[s : s + 1], (128, 128)).T

    kv_right_in(0)
    kv_right(1)
    kv_left_in(0)
    kv_left(1)
    arrived(enc_w.at[:, left, core], S_ENC_W)
    to(enc_w.at[0, left, core], S_ENC_W + 2, (c, n, right))
    to(enc_w.at[:, left, core], S_ENC_W + 4, (mate, n, t))
    arrived(enc_w.at[:, right, core], S_ENC_W + 1)
    to(enc_w.at[1, right, core], S_ENC_W + 3, (c, n, left))
    to(enc_w.at[:, right, core], S_ENC_W + 5, (mate, n, t))
    kv_right_in(1)
    kv_right(2)
    kv_left_in(1)
    kv_left(2)

    for k in range(2):
        other = first + 4 * k

        @pl.when(other != n)
        def _():
            arrived(emb.at[k], S_EMB + k)

        @pl.when(other == n)
        def _():
            pltpu.make_async_copy(embed.at[n], emb.at[k], local.at[4]).wait()

        normed[k] = norm_rows(emb[k].astype(jnp.float32), gain_in[...].astype(jnp.float32).reshape(1, 768))

    def encode_heads(shard):
        query = dot(enc_w[0, shard].reshape(192, 768), normed[...].reshape(256, 768), NT)
        query = query.astype(jnp.bfloat16) * jnp.bfloat16(EHD ** (-0.5))
        columns = []
        for k in range(2):
            rows = []
            for h in range(3):
                at = slice(h * EHD, (h + 1) * EHD)
                both = cond[shard, k, at, :]
                scores = dot(both, query[at, k * 128 : (k + 1) * 128], TN)[:STRETCH_TOKENS]
                raised = jnp.exp(scores - jnp.max(scores, axis=0, keepdims=True))
                weights = (raised / jnp.sum(raised, axis=0, keepdims=True)).astype(jnp.bfloat16)
                spread = jnp.concatenate([jnp.zeros_like(weights), weights], axis=0)
                rows.append(dot(both, spread, NN).astype(jnp.bfloat16))
            columns.append(jnp.concatenate(rows, axis=0))
        mixed[shard] = jnp.concatenate(columns, axis=1)

    encode_heads(t)
    arrived(enc_w.at[0, across, core], S_ENC_W + 2)
    to(enc_w.at[0, across, core], S_ENC_W + 6, (mate, n, t))
    arrived(enc_w.at[1, across, core], S_ENC_W + 3)
    to(enc_w.at[1, across, core], S_ENC_W + 7, (mate, n, t))
    out_right_in(0)
    out_right(1)
    out_left_in(0)
    out_left(1)
    arrived(cond.at[left], S_COND)
    arrived(enc_w.at[:, left, 1 - core], S_ENC_W + 4)
    encode_heads(left)
    kv_right_in(2)
    kv_right(3)
    kv_left_in(2)
    arrived(cond.at[right], S_COND + 2)
    arrived(enc_w.at[:, right, 1 - core], S_ENC_W + 5)
    encode_heads(right)
    arrived(cond.at[across], S_COND + 1)
    arrived(enc_w.at[0, across, 1 - core], S_ENC_W + 6)
    encode_heads(across)
    arrived(enc_w.at[1, across, 1 - core], S_ENC_W + 7)

    updated = dot(mixed[...].reshape(768, 256), enc_w[1].reshape(768, 768), TN)
    gain = gain_out[...].astype(jnp.float32).reshape(1, 768)
    for k in range(2):
        rows = emb[k].astype(jnp.float32) + updated[k * 128 : (k + 1) * 128]
        encoded[first + 4 * k] = norm_rows(rows, gain)

    for k in range(2):
        to(encoded.at[first + 4 * k], S_AG + 2 * k, (c, n, right))
        to(encoded.at[first + 4 * k], S_AG + 2 * k + 1, (c, n, left))

    kv_right_in(3)
    to(kv_w.at[:, :, core], S_KV_MATE, (mate, n, t))
    out_right_in(1)
    out_right(2)
    out_left_in(1)
    out_left(2)
    arrived(kv_w.at[:, :, 1 - core], S_KV_MATE)

    def project(rows):
        made = []
        for i in range(2):
            made.append(dot(rows, kv_w[i].reshape(768, 512), NN).astype(jnp.bfloat16))
        return made

    def project_pair(start):
        rows = jnp.concatenate([encoded[start], encoded[start + 4]], axis=0)
        got_k, got_v = project(rows)
        for k in range(2):
            keys[start + 4 * k] = got_k[k * 128 : (k + 1) * 128]
            values[start + 4 * k] = got_v[k * 128 : (k + 1) * 128]

    def first_of(shard):
        return lax.rem(shard - n + 8, 4)

    project_pair(first)
    arrived(encoded.at[first_of(left)], S_AG)
    to(encoded.at[first_of(left)], S_AG + 4, (c, n, right))
    arrived(encoded.at[first_of(right) + 4], S_AG + 3)
    to(encoded.at[first_of(right) + 4], S_AG + 5, (c, n, left))
    arrived(encoded.at[first_of(left) + 4], S_AG + 2)
    project_pair(first_of(left))
    arrived(encoded.at[first_of(right)], S_AG + 1)
    project_pair(first_of(right))
    out_right_in(2)
    out_right(3)
    out_left_in(2)
    arrived(encoded.at[first_of(across)], S_AG + 4)
    arrived(encoded.at[first_of(across) + 4], S_AG + 5)

    project_pair(first_of(across))

    slot_of = []
    for s in range(8):
        place = jnp.int32(0)
        for o in range(1, 8):
            place = jnp.where(slots[o, block] == s, o, place)
        slot_of.append(place)

    lane = lax.broadcasted_iota(jnp.int32, (1, 128), 1)
    use_lane = (lane >= STRETCH_TOKENS - 1) & (lane < 2 * STRETCH_TOKENS - 1)

    def attend(st, h, query_rows):
        at = slice(h * HEAD_WIDTH, (h + 1) * HEAD_WIDTH)
        pair = (slot_of[2 * st], slot_of[2 * st + 1])
        key_rows = jnp.concatenate([keys[p, :, at] for p in pair], axis=0)
        value_rows = jnp.concatenate([values[p, :, at] for p in pair], axis=0)
        allowed = key_mask[2 * st : 2 * st + 2].reshape(256, 128)
        scores = dot(key_rows, query_rows, NT) * HEAD_WIDTH ** (-0.5)
        scores = jnp.where(allowed > 0, scores, -1e30)
        raised = jnp.exp(scores - jnp.max(scores, axis=0, keepdims=True)) * allowed
        sums = jnp.sum(raised, axis=0, keepdims=True)
        use = (sums > 0) & use_lane
        share = jnp.where(use, 1.0 / jnp.where(use, sums, 1.0), 0.0)
        return dot((raised * share).astype(jnp.bfloat16), value_rows, TN)

    heads = [slice(h * HEAD_WIDTH, (h + 1) * HEAD_WIDTH) for h in range(4)]
    arrived(queries_next, S_QUERY)
    fourth = []
    for h, at in enumerate(heads):
        got = attend(3, h, jnp.concatenate([queries[192:256, at], queries_next[:, at]], axis=0))
        rows_send[:, at] = got[64:].astype(jnp.bfloat16)
        fourth.append(got[:64])
    to(rows_send, S_PREV, next_device, dst=rows_got)

    second = []
    for h, at in enumerate(heads):
        three = attend(2, h, queries[128:256, at])
        two = attend(1, h, queries[64:192, at])
        lower = jnp.concatenate([two[64:] + three[:64], three[64:] + fourth[h]], axis=0)
        attended[t, 128:256, at] = lower.astype(jnp.bfloat16)
        second.append(two[:64])

    def piece(half, shard):
        return attended.at[shard, pl.ds(128 * half, 128)]

    to(piece(1, t), S_ATT, (c, n, right))
    to(piece(1, t), S_ATT + 1, (c, n, left))

    ones = [attend(0, h, queries[0:128, at]) for h, at in enumerate(heads)]
    arrived(rows_got, S_PREV)
    for h, at in enumerate(heads):
        before_rows = jnp.where(block > 0, rows_got[:, at].astype(jnp.float32), 0.0)
        upper = jnp.concatenate([ones[h][:64] + before_rows, ones[h][64:] + second[h]], axis=0)
        attended[t, 0:128, at] = upper.astype(jnp.bfloat16)
    to(piece(0, t), S_ATT + 2, (c, n, right))
    to(piece(0, t), S_ATT + 3, (c, n, left))

    out_right_in(3)
    for i in range(8):
        at = y if i == 0 else (y - i + 8 if i < 5 else y + i - 4)
        arrived(w_out.at[lax.rem(at, 8), 1 - core], S_OUT_MATE + i)
    own[9].wait()

    def product(shard):
        return dot(attended[shard], w_out[pl.ds(2 * shard, 2)].reshape(512, 1024), NN)

    arrived(piece(1, left), S_ATT)
    to(piece(1, left), S_ATT + 4, (c, n, right))
    total[...] = hidden[...].astype(jnp.float32) + product(t)
    arrived(piece(0, right), S_ATT + 3)
    to(piece(0, right), S_ATT + 5, (c, n, left))
    arrived(piece(0, left), S_ATT + 2)
    total[...] += product(left)
    arrived(piece(1, right), S_ATT + 1)
    total[...] += product(right)
    arrived(piece(1, across), S_ATT + 4)
    arrived(piece(0, across), S_ATT + 5)
    output[...] = (total[...] + product(across)).astype(jnp.bfloat16)

    for k in range(2):

        @pl.when(first + 4 * k != n)
        def _():
            emb_copy(k).wait_send()

    for made in sent:
        made.wait_send()


def per_device(
    hidden,
    queries,
    key_weight_matrix,
    value_weight_matrix,
    w_out,
    neighbour_embed,
    neighbour_ids,
    neighbour_count,
    slot_seq,
    cond_keys,
    cond_values,
    enc_gain,
    enc_query,
    enc_out,
    final_gain,
):
    vmem, hbm = pl.BlockSpec(memory_space=pltpu.VMEM), pl.BlockSpec(memory_space=pltpu.HBM)
    smem = pl.BlockSpec(memory_space=pltpu.SMEM)
    bf16, f32 = jnp.bfloat16, jnp.float32
    return pl.pallas_call(
        body,
        out_shape=jax.ShapeDtypeStruct((256, 1024), bf16),
        in_specs=[smem, smem, *[hbm] * 11, vmem, vmem],
        out_specs=vmem,
        scratch_shapes=[
            pltpu.VMEM((192, 256), bf16),
            pltpu.VMEM((192, 256), bf16),
            pltpu.VMEM((256, 512), bf16),
            pltpu.VMEM((8, 128), jnp.int32),
            pltpu.VMEM((8, 2, 128, 1024), bf16),
            pltpu.VMEM((256, 1024), bf16),
            pltpu.VMEM((256, 1024), f32),
            pltpu.VMEM((4, 256, 512), bf16),
            pltpu.VMEM((64, 512), bf16),
            pltpu.VMEM((64, 512), bf16),
            pltpu.VMEM((64, 512), bf16),
            pltpu.VMEM((2, 128, 768), bf16),
            pltpu.VMEM((4, 192, 128), bf16),
            pltpu.VMEM((3, 2, 192, 128), bf16),
            pltpu.VMEM((4, 2, 192, 128), bf16),
            pltpu.VMEM((2, 4, 2, 96, 768), bf16),
            pltpu.VMEM((2, 128, 768), bf16),
            pltpu.VMEM((4, 192, 256), bf16),
            pltpu.VMEM((8, 128, 768), bf16),
            pltpu.VMEM((2, 8, 2, 48, 512), bf16),
            pltpu.VMEM((8, 128, 512), bf16),
            pltpu.VMEM((8, 128, 512), bf16),
            pltpu.VMEM((8, 128, 128), f32),
            pltpu.SemaphoreType.DMA((N_SEMS,)),
            pltpu.SemaphoreType.DMA((N_SEMS,)),
            pltpu.SemaphoreType.DMA((11,)),
        ],
        compiler_params=pltpu.CompilerParams(
            collective_id=0, has_side_effects=True, vmem_limit_bytes=62 * 2**20
        ),
        cost_estimate=pl.CostEstimate(flops=4 * 10**9, bytes_accessed=150 * 10**6, transcendentals=0),
    )(
        slot_seq.T,
        neighbour_count,
        neighbour_embed,
        cond_keys.T,
        cond_values.T,
        enc_query.T.reshape(2, 96, 768),
        enc_out.reshape(2, 96, 768),
        key_weight_matrix,
        value_weight_matrix,
        queries,
        neighbour_ids,
        w_out,
        hidden,
        enc_gain,
        final_gain,
    )


def solution(mesh):
    in_specs = (
        P(("ctx", "nbr"), "tp"),
        P(("ctx", "nbr"), "tp"),
        P("ctx", "tp"),
        P("ctx", "tp"),
        P("ctx", "tp"),
        P(("ctx", "nbr"), None, None),
        P(("ctx", "nbr"), None),
        P(("ctx", "nbr")),
        P(),
        P(("ctx", "nbr"), "tp"),
        P(("ctx", "nbr"), "tp"),
        P(),
        P(None, "tp"),
        P("tp", None),
        P(),
    )
    out_specs = P(("ctx", "nbr"), "tp")
    return jax.shard_map(
        per_device, mesh=mesh, in_specs=in_specs, out_specs=out_specs, check_vma=False
    )
```

```python
import jax
import jax.numpy as jnp
from jax import lax
from jax.experimental import pallas as pl
from jax.experimental.pallas import tpu as pltpu
from jax.sharding import PartitionSpec as P

HEAD_WIDTH = 128
EHD = 64
STRETCH_TOKENS = 64
NEIGHBOUR_TOKENS = 128
EPSILON = 1e-06
MESH = pl.DeviceIdType.MESH
NT = (((1,), (1,)), ((), ()))
TN = (((0,), (0,)), ((), ()))
NN = (((1,), (0,)), ((), ()))

S_EMB, S_COND, S_ENC_Q, S_ENC_O, S_KV_RIGHT, S_KV_LEFT, S_KV_MATE, S_QUERY, S_AG, S_PREV = (
    0, 2, 6, 14, 22, 26, 29, 30, 31, 37,
)
S_OUT_RIGHT, S_OUT_LEFT, S_OUT_MATE, S_ATT = 38, 42, 45, 53
N_SEMS = 65


def dot(a, b, dims):
    return lax.dot_general(a, b, dims, preferred_element_type=jnp.float32)


def norm_rows(rows, gain):
    scale = lax.rsqrt(jnp.mean(rows * rows, axis=-1, keepdims=True) + EPSILON)
    return (rows * scale * gain).astype(jnp.bfloat16)


def body(
    slots, counts, embed, cond_k_far, cond_v_far, enc_q, enc_o, key_w, value_w, queries_far, ids_far, w_far, hidden_far,
    gain_in, gain_out,
    output,
    cond_k, cond_v, queries, ids, w_out, hidden, total, attended, queries_next, rows_send, rows_got,
    emb, packs, cond_send, cond_own, cond_side, cond_across, enc_w, normed, mixed, encoded, kv_w, keys, values, key_mask, send, recv, local,
):
    c, n, t = lax.axis_index("ctx"), lax.axis_index("nbr"), lax.axis_index("tp")
    block = c * 8 + n
    right, left, across = lax.rem(t + 1, 4), lax.rem(t + 3, 4), lax.rem(t + 2, 4)
    core = lax.rem(c, 2)
    y = c // 2
    mate = c + 1 - 2 * core
    c_right, c_left = lax.rem(c + 2, 16), lax.rem(c + 14, 16)
    first = lax.rem(t - n + 8, 4)
    nxt = lax.rem(block + 1, 128)
    before = lax.rem(block + 127, 128)
    next_device = (nxt // 8, lax.rem(nxt, 8), t)
    before_device = (before // 8, lax.rem(before, 8), t)

    def copy(src, dst, s, r, device):
        return pltpu.make_async_remote_copy(
            src_ref=src, dst_ref=dst, send_sem=send.at[s], recv_sem=recv.at[r],
            device_id=device, device_id_type=MESH,
        )

    def to(ref, s, device, dst=None, r=None):
        made = copy(ref, ref if dst is None else dst, s, s if r is None else r, device)
        made.start()
        sent.append(made)

    def arrived(ref, r):
        copy(ref, ref, r, r, (c, n, right)).wait_recv()

    sent = []

    own = [
        pltpu.make_async_copy(enc_q, enc_w.at[0, t], local.at[0]),
        pltpu.make_async_copy(enc_o, enc_w.at[1, t], local.at[1]),
        pltpu.make_async_copy(key_w, kv_w.at[0, y, core], local.at[2]),
        pltpu.make_async_copy(value_w, kv_w.at[1, y, core], local.at[3]),
        pltpu.make_async_copy(cond_k_far, cond_k, local.at[5]),
        pltpu.make_async_copy(cond_v_far, cond_v, local.at[6]),
        pltpu.make_async_copy(queries_far, queries, local.at[7]),
        pltpu.make_async_copy(ids_far, ids, local.at[8]),
        pltpu.make_async_copy(w_far, w_out.at[y, core], local.at[9]),
        pltpu.make_async_copy(hidden_far, hidden, local.at[10]),
    ]
    for made in own:
        made.start()

    barrier = pltpu.get_barrier_semaphore()
    for device in (
        (c, n, right), (c, n, left), (c, n, across), (mate, n, t), (c_right, n, t), (c_left, n, t), before_device,
        next_device,
    ):
        pl.semaphore_signal(barrier, inc=1, device_id=device, device_id_type=MESH)
    for k in range(2):
        other = first + 4 * k

        @pl.when(other != n)
        def _():
            pl.semaphore_signal(barrier, inc=1, device_id=(c, other, t), device_id_type=MESH)

    with_self = jnp.where(lax.rem(2 * n, 4) == t, 1, 0)
    pl.semaphore_wait(barrier, 10 - with_self)

    mine = n // 4

    def emb_copy(k):
        other = first + 4 * k
        return copy(embed.at[other], emb.at[mine], S_EMB + k, S_EMB + mine, (c, other, t))

    for k in range(2):
        other = first + 4 * k

        @pl.when(other != n)
        def _():
            emb_copy(k).start()

        @pl.when(other == n)
        def _():
            pltpu.make_async_copy(embed.at[n], emb.at[mine], local.at[4]).start()

    def enc_half(i, shard, of=None, part=None):
        rows = enc_w.at[i, shard, core if of is None else of]
        return rows if part is None else rows.at[pl.ds(48 * part, 48)]

    enc_sem = (S_ENC_Q, S_ENC_O)

    def enc_send(i):
        source = (enc_q, enc_o)[i].at[core]
        to(source, enc_sem[i], (c, n, right), dst=enc_half(i, t))
        to(source, enc_sem[i] + 1, (c, n, left), dst=enc_half(i, t))

    def enc_pass_on(i):
        arrived(enc_half(i, left), enc_sem[i])
        to(enc_half(i, left, part=0), enc_sem[i] + 2, (c, n, right))
        to(enc_half(i, left), enc_sem[i] + 4, (mate, n, t))
        arrived(enc_half(i, right), enc_sem[i] + 1)
        to(enc_half(i, right, part=1), enc_sem[i] + 3, (c, n, left))
        to(enc_half(i, right), enc_sem[i] + 5, (mate, n, t))

    def enc_last(i):
        for part in range(2):
            arrived(enc_half(i, across, part=part), enc_sem[i] + 2 + part)
            to(enc_half(i, across, part=part), enc_sem[i] + 6 + part, (mate, n, t))

    def enc_mate(i, shard, at):
        arrived(enc_half(i, shard, 1 - core), enc_sem[i] + at)

    def enc_mate_across(i):
        for part in range(2):
            arrived(enc_half(i, across, 1 - core, part), enc_sem[i] + 6 + part)

    enc_send(0)

    own[2].wait()
    own[3].wait()

    def kv_right(s):
        to(kv_w.at[:, lax.rem(y - s + 8, 8), core], S_KV_RIGHT + s, (c_right, n, t))

    def kv_left(s):
        to(kv_w.at[:, lax.rem(y + s, 8), core], S_KV_LEFT + s, (c_left, n, t))

    def kv_right_in(s):
        arrived(kv_w.at[:, lax.rem(y - s - 1 + 8, 8), core], S_KV_RIGHT + s)

    def kv_left_in(s):
        arrived(kv_w.at[:, lax.rem(y + s + 1, 8), core], S_KV_LEFT + s)

    def out_right(s):
        to(w_out.at[lax.rem(y - s + 8, 8), core], S_OUT_RIGHT + s, (c_right, n, t))

    def out_left(s):
        to(w_out.at[lax.rem(y + s, 8), core], S_OUT_LEFT + s, (c_left, n, t))

    def out_right_in(s):
        arrived(w_out.at[lax.rem(y - s - 1 + 8, 8), core], S_OUT_RIGHT + s)
        to(w_out.at[lax.rem(y - s - 1 + 8, 8), core], S_OUT_MATE + 1 + s, (mate, n, t))

    def out_left_in(s):
        arrived(w_out.at[lax.rem(y + s + 1, 8), core], S_OUT_LEFT + s)
        to(w_out.at[lax.rem(y + s + 1, 8), core], S_OUT_MATE + 5 + s, (mate, n, t))

    kv_right(0)
    kv_left(0)

    own[4].wait()
    own[5].wait()
    for st in range(4):
        at = slice(st * STRETCH_TOKENS, (st + 1) * STRETCH_TOKENS)
        packs[st] = jnp.concatenate([cond_k[:, at], cond_v[:, at]], axis=1)
    def pack_for(shard, k):
        return packs[slots[lax.rem(shard - n + 8, 4) + 4 * k, block] // 2]

    for side, device in enumerate((right, left)):
        for k in range(2):
            cond_send[side, k] = pack_for(device, k)
        cond_send[side, 2] = pack_for(across, side)
        to(cond_send.at[side], S_COND + side, (c, n, device), dst=cond_side.at[side])
    for k in range(2):
        cond_own[k] = pack_for(t, k)

    own[6].wait()
    to(queries.at[pl.ds(0, STRETCH_TOKENS)], S_QUERY, before_device, dst=queries_next)
    own[8].wait()
    out_right(0)
    out_left(0)
    to(w_out.at[y, core], S_OUT_MATE, (mate, n, t))

    own[7].wait()
    row = lax.broadcasted_iota(jnp.int32, (8, 128), 0)
    count = jnp.zeros((8, 128), jnp.int32)
    for st in range(4):
        count = jnp.where(row // 2 == st, counts[st], count)
    mask = jnp.where((lax.rem(row, 2) < count) & (ids[...] != 0), 1.0, 0.0)
    for s in range(8):
        key_mask[s] = jnp.broadcast_to(mask[s : s + 1], (128, 128)).T

    kv_right_in(0)
    kv_right(1)
    kv_left_in(0)
    kv_left(1)
    enc_pass_on(0)
    enc_send(1)
    for side, device in enumerate((right, left)):
        arrived(cond_side.at[side], S_COND + side)
        to(cond_side.at[side, 2], S_COND + 2 + side, (c, n, device), dst=cond_across.at[side])
    kv_right_in(1)
    kv_right(2)
    kv_left_in(1)
    kv_left(2)

    for k in range(2):
        other = first + 4 * k

        @pl.when(other != n)
        def _():
            arrived(emb.at[k], S_EMB + k)

        @pl.when(other == n)
        def _():
            pltpu.make_async_copy(embed.at[n], emb.at[k], local.at[4]).wait()

        normed[k] = norm_rows(emb[k].astype(jnp.float32), gain_in[...].astype(jnp.float32).reshape(1, 768))

    own[0].wait()
    own[1].wait()
    enc_last(0)

    def encode_heads(shard, states):
        query = dot(enc_w[0, shard].reshape(192, 768), normed[...].reshape(256, 768), NT)
        query = query.astype(jnp.bfloat16) * jnp.bfloat16(EHD ** (-0.5))
        columns = []
        for k in range(2):
            rows = []
            for h in range(3):
                at = slice(h * EHD, (h + 1) * EHD)
                both = states[k, at, :]
                scores = dot(both, query[at, k * 128 : (k + 1) * 128], TN)[:STRETCH_TOKENS]
                raised = jnp.exp(scores - jnp.max(scores, axis=0, keepdims=True))
                weights = (raised / jnp.sum(raised, axis=0, keepdims=True)).astype(jnp.bfloat16)
                spread = jnp.concatenate([jnp.zeros_like(weights), weights], axis=0)
                rows.append(dot(both, spread, NN).astype(jnp.bfloat16))
            columns.append(jnp.concatenate(rows, axis=0))
        mixed[shard] = jnp.concatenate(columns, axis=1)

    encode_heads(t, cond_own)
    enc_mate(0, left, 4)
    encode_heads(left, cond_side.at[0])
    enc_pass_on(1)
    out_right_in(0)
    out_right(1)
    out_left_in(0)
    out_left(1)
    enc_mate(0, right, 5)
    encode_heads(right, cond_side.at[1])
    kv_right_in(2)
    kv_right(3)
    kv_left_in(2)
    for side in range(2):
        arrived(cond_across.at[side], S_COND + 2 + side)
    enc_mate_across(0)
    encode_heads(across, cond_across)
    enc_last(1)
    enc_mate(1, left, 4)
    enc_mate(1, right, 5)
    enc_mate_across(1)

    gain = gain_out[...].astype(jnp.float32).reshape(1, 768)
    for k in range(2):
        heads_out = mixed[:, :, k * 128 : (k + 1) * 128].reshape(768, 128)
        updated = dot(heads_out, enc_w[1].reshape(768, 768), TN)
        encoded[first + 4 * k] = norm_rows(emb[k].astype(jnp.float32) + updated, gain)
        to(encoded.at[first + 4 * k], S_AG + 2 * k, (c, n, right))
        to(encoded.at[first + 4 * k], S_AG + 2 * k + 1, (c, n, left))

    kv_right_in(3)
    to(kv_w.at[:, :, core], S_KV_MATE, (mate, n, t))
    out_right_in(1)
    out_right(2)
    out_left_in(1)
    out_left(2)
    arrived(kv_w.at[:, :, 1 - core], S_KV_MATE)

    def project(rows):
        made = []
        for i in range(2):
            made.append(dot(rows, kv_w[i].reshape(768, 512), NN).astype(jnp.bfloat16))
        return made

    def project_pair(start):
        rows = jnp.concatenate([encoded[start], encoded[start + 4]], axis=0)
        got_k, got_v = project(rows)
        for k in range(2):
            keys[start + 4 * k] = got_k[k * 128 : (k + 1) * 128]
            values[start + 4 * k] = got_v[k * 128 : (k + 1) * 128]

    def first_of(shard):
        return lax.rem(shard - n + 8, 4)

    project_pair(first)
    arrived(encoded.at[first_of(left)], S_AG)
    to(encoded.at[first_of(left)], S_AG + 4, (c, n, right))
    arrived(encoded.at[first_of(right) + 4], S_AG + 3)
    to(encoded.at[first_of(right) + 4], S_AG + 5, (c, n, left))
    arrived(encoded.at[first_of(left) + 4], S_AG + 2)
    project_pair(first_of(left))
    arrived(encoded.at[first_of(right)], S_AG + 1)
    project_pair(first_of(right))
    out_right_in(2)
    out_right(3)
    out_left_in(2)
    arrived(encoded.at[first_of(across)], S_AG + 4)
    arrived(encoded.at[first_of(across) + 4], S_AG + 5)

    project_pair(first_of(across))

    slot_of = []
    for s in range(8):
        place = jnp.int32(0)
        for o in range(1, 8):
            place = jnp.where(slots[o, block] == s, o, place)
        slot_of.append(place)

    lane = lax.broadcasted_iota(jnp.int32, (1, 128), 1)
    use_lane = (lane >= STRETCH_TOKENS - 1) & (lane < 2 * STRETCH_TOKENS - 1)

    def attend(st, h, query_rows):
        at = slice(h * HEAD_WIDTH, (h + 1) * HEAD_WIDTH)
        pair = (slot_of[2 * st], slot_of[2 * st + 1])
        key_rows = jnp.concatenate([keys[p, :, at] for p in pair], axis=0)
        value_rows = jnp.concatenate([values[p, :, at] for p in pair], axis=0)
        allowed = key_mask[2 * st : 2 * st + 2].reshape(256, 128)
        scores = dot(key_rows, query_rows, NT) * HEAD_WIDTH ** (-0.5)
        scores = jnp.where(allowed > 0, scores, -1e30)
        raised = jnp.exp(scores - jnp.max(scores, axis=0, keepdims=True)) * allowed
        sums = jnp.sum(raised, axis=0, keepdims=True)
        use = (sums > 0) & use_lane
        share = jnp.where(use, 1.0 / jnp.where(use, sums, 1.0), 0.0)
        return dot((raised * share).astype(jnp.bfloat16), value_rows, TN)

    heads = [slice(h * HEAD_WIDTH, (h + 1) * HEAD_WIDTH) for h in range(4)]
    arrived(queries_next, S_QUERY)
    fourth = []
    for h, at in enumerate(heads):
        got = attend(3, h, jnp.concatenate([queries[192:256, at], queries_next[:, at]], axis=0))
        rows_send[:, at] = got[64:].astype(jnp.bfloat16)
        fourth.append(got[:64])
    to(rows_send, S_PREV, next_device, dst=rows_got)

    def piece(i, shard):
        return attended.at[shard, pl.ds(STRETCH_TOKENS * (3 - i), STRETCH_TOKENS)]

    def leave(i, rows):
        for h, at in enumerate(heads):
            attended[t, 64 * (3 - i) : 64 * (4 - i), at] = rows[h].astype(jnp.bfloat16)
        to(piece(i, t), S_ATT + 3 * i, (c, n, right))
        to(piece(i, t), S_ATT + 3 * i + 1, (c, n, left))

    def pass_on(i):
        if i % 2 == 0:
            arrived(piece(i, left), S_ATT + 3 * i)
            to(piece(i, left), S_ATT + 3 * i + 2, (c, n, right))
        else:
            arrived(piece(i, right), S_ATT + 3 * i + 1)
            to(piece(i, right), S_ATT + 3 * i + 2, (c, n, left))

    after = fourth
    for i, st in enumerate((2, 1, 0)):
        got = [attend(st, h, queries[64 * st : 64 * st + 128, at]) for h, at in enumerate(heads)]
        leave(i, [got[h][64:] + after[h] for h in range(4)])
        after = [rows[:64] for rows in got]
        if i > 0:
            pass_on(i - 1)
    arrived(rows_got, S_PREV)
    leave(3, [after[h] + jnp.where(block > 0, rows_got[:, at].astype(jnp.float32), 0.0) for h, at in enumerate(heads)])
    pass_on(2)

    out_right_in(3)
    for i in range(8):
        at = y if i == 0 else (y - i + 8 if i < 5 else y + i - 4)
        arrived(w_out.at[lax.rem(at, 8), 1 - core], S_OUT_MATE + i)
    own[9].wait()

    def product(shard, rows=slice(0, 256)):
        return dot(attended[shard, rows], w_out[pl.ds(2 * shard, 2)].reshape(512, 1024), NN)

    total[...] = hidden[...].astype(jnp.float32) + product(t)
    pass_on(3)
    for i in (1, 3):
        arrived(piece(i, left), S_ATT + 3 * i)
    total[...] += product(left)
    for i in (0, 2):
        arrived(piece(i, right), S_ATT + 3 * i + 1)
    total[...] += product(right)
    for half in range(2):
        for i in (2 * half, 2 * half + 1):
            arrived(piece(i, across), S_ATT + 3 * i + 2)
        rows = slice(128 - 128 * half, 256 - 128 * half)
        output[rows] = (total[rows] + product(across, rows)).astype(jnp.bfloat16)

    for k in range(2):

        @pl.when(first + 4 * k != n)
        def _():
            emb_copy(k).wait_send()

    for made in sent:
        made.wait_send()


def per_device(
    hidden,
    queries,
    key_weight_matrix,
    value_weight_matrix,
    w_out,
    neighbour_embed,
    neighbour_ids,
    neighbour_count,
    slot_seq,
    cond_keys,
    cond_values,
    enc_gain,
    enc_query,
    enc_out,
    final_gain,
):
    vmem, hbm = pl.BlockSpec(memory_space=pltpu.VMEM), pl.BlockSpec(memory_space=pltpu.HBM)
    smem = pl.BlockSpec(memory_space=pltpu.SMEM)
    bf16, f32 = jnp.bfloat16, jnp.float32
    return pl.pallas_call(
        body,
        out_shape=jax.ShapeDtypeStruct((256, 1024), bf16),
        in_specs=[smem, smem, *[hbm] * 11, vmem, vmem],
        out_specs=vmem,
        scratch_shapes=[
            pltpu.VMEM((192, 256), bf16),
            pltpu.VMEM((192, 256), bf16),
            pltpu.VMEM((256, 512), bf16),
            pltpu.VMEM((8, 128), jnp.int32),
            pltpu.VMEM((8, 2, 128, 1024), bf16),
            pltpu.VMEM((256, 1024), bf16),
            pltpu.VMEM((256, 1024), f32),
            pltpu.VMEM((4, 256, 512), bf16),
            pltpu.VMEM((64, 512), bf16),
            pltpu.VMEM((64, 512), bf16),
            pltpu.VMEM((64, 512), bf16),
            pltpu.VMEM((2, 128, 768), bf16),
            pltpu.VMEM((4, 192, 128), bf16),
            pltpu.VMEM((2, 3, 192, 128), bf16),
            pltpu.VMEM((2, 192, 128), bf16),
            pltpu.VMEM((2, 3, 192, 128), bf16),
            pltpu.VMEM((2, 192, 128), bf16),
            pltpu.VMEM((2, 4, 2, 96, 768), bf16),
            pltpu.VMEM((2, 128, 768), bf16),
            pltpu.VMEM((4, 192, 256), bf16),
            pltpu.VMEM((8, 128, 768), bf16),
            pltpu.VMEM((2, 8, 2, 48, 512), bf16),
            pltpu.VMEM((8, 128, 512), bf16),
            pltpu.VMEM((8, 128, 512), bf16),
            pltpu.VMEM((8, 128, 128), f32),
            pltpu.SemaphoreType.DMA((N_SEMS,)),
            pltpu.SemaphoreType.DMA((N_SEMS,)),
            pltpu.SemaphoreType.DMA((11,)),
        ],
        compiler_params=pltpu.CompilerParams(
            collective_id=0, has_side_effects=True, vmem_limit_bytes=62 * 2**20
        ),
        cost_estimate=pl.CostEstimate(flops=4 * 10**9, bytes_accessed=150 * 10**6, transcendentals=0),
    )(
        slot_seq.T,
        neighbour_count,
        neighbour_embed,
        cond_keys.T,
        cond_values.T,
        enc_query.T.reshape(2, 96, 768),
        enc_out.reshape(2, 96, 768),
        key_weight_matrix,
        value_weight_matrix,
        queries,
        neighbour_ids,
        w_out,
        hidden,
        enc_gain,
        final_gain,
    )


def solution(mesh):
    in_specs = (
        P(("ctx", "nbr"), "tp"),
        P(("ctx", "nbr"), "tp"),
        P("ctx", "tp"),
        P("ctx", "tp"),
        P("ctx", "tp"),
        P(("ctx", "nbr"), None, None),
        P(("ctx", "nbr"), None),
        P(("ctx", "nbr")),
        P(),
        P(("ctx", "nbr"), "tp"),
        P(("ctx", "nbr"), "tp"),
        P(),
        P(None, "tp"),
        P("tp", None),
        P(),
    )
    out_specs = P(("ctx", "nbr"), "tp")
    return jax.shard_map(
        per_device, mesh=mesh, in_specs=in_specs, out_specs=out_specs, check_vma=False
    )
```

```python
import jax
import jax.numpy as jnp
from jax import lax
from jax.experimental import pallas as pl
from jax.experimental.pallas import tpu as pltpu
from jax.sharding import PartitionSpec as P

HEAD_WIDTH = 128
EHD = 64
STRETCH_TOKENS = 64
NEIGHBOUR_TOKENS = 128
EPSILON = 1e-06
MESH = pl.DeviceIdType.MESH
NT = (((1,), (1,)), ((), ()))
TN = (((0,), (0,)), ((), ()))
NN = (((1,), (0,)), ((), ()))

S_EMB, S_COND, S_ENC_W, S_KV_RIGHT, S_KV_LEFT, S_KV_MATE, S_QUERY, S_AG, S_PREV, S_ATT = (
    0, 2, 5, 13, 17, 20, 21, 22, 28, 29,
)
S_OUT_RIGHT, S_OUT_LEFT, S_OUT_MATE = 41, 45, 48
S_COND_LAST = 56
N_SEMS = 57


def dot(a, b, dims):
    return lax.dot_general(a, b, dims, preferred_element_type=jnp.float32)


def norm_rows(rows, gain):
    scale = lax.rsqrt(jnp.mean(rows * rows, axis=-1, keepdims=True) + EPSILON)
    return (rows * scale * gain).astype(jnp.bfloat16)


def body(
    slots, counts, embed, cond_k_far, cond_v_far, enc_q, enc_o, key_w, value_w, queries_far, ids_far, w_far, hidden_far,
    gain_in, gain_out,
    output,
    cond_k, cond_v, queries, ids, w_out, hidden, total, attended, queries_next, rows_send, rows_got,
    emb, packs, cond_send, cond_own, cond_side, cond_across, enc_w, normed, mixed, encoded, kv_w, keys, values, key_mask, send, recv, local, ready,
):
    c, n, t = lax.axis_index("ctx"), lax.axis_index("nbr"), lax.axis_index("tp")
    block = c * 8 + n
    right, left, across = lax.rem(t + 1, 4), lax.rem(t + 3, 4), lax.rem(t + 2, 4)
    core = lax.rem(c, 2)
    y = c // 2
    mate = c + 1 - 2 * core
    c_right, c_left = lax.rem(c + 2, 16), lax.rem(c + 14, 16)
    first = lax.rem(t - n + 8, 4)
    nxt = lax.rem(block + 1, 128)
    before = lax.rem(block + 127, 128)
    next_device = (nxt // 8, lax.rem(nxt, 8), t)
    before_device = (before // 8, lax.rem(before, 8), t)

    def copy(src, dst, s, r, device):
        return pltpu.make_async_remote_copy(
            src_ref=src, dst_ref=dst, send_sem=send.at[s], recv_sem=recv.at[r],
            device_id=device, device_id_type=MESH,
        )

    def to(ref, s, device, dst=None, r=None):
        made = copy(ref, ref if dst is None else dst, s, s if r is None else r, device)
        made.start()
        sent.append(made)

    def arrived(ref, r):
        copy(ref, ref, r, r, (c, n, right)).wait_recv()

    sent = []

    own = [
        pltpu.make_async_copy(enc_q, enc_w.at[0, t], local.at[0]),
        pltpu.make_async_copy(enc_o, enc_w.at[1, t], local.at[1]),
        pltpu.make_async_copy(key_w, kv_w.at[0, y, core], local.at[2]),
        pltpu.make_async_copy(value_w, kv_w.at[1, y, core], local.at[3]),
        pltpu.make_async_copy(cond_k_far, cond_k, local.at[5]),
        pltpu.make_async_copy(cond_v_far, cond_v, local.at[6]),
        pltpu.make_async_copy(queries_far, queries, local.at[7]),
        pltpu.make_async_copy(ids_far, ids, local.at[8]),
        pltpu.make_async_copy(w_far, w_out.at[y, core], local.at[9]),
        pltpu.make_async_copy(hidden_far, hidden, local.at[10]),
    ]
    for made in own:
        made.start()

    barrier = pltpu.get_barrier_semaphore()
    others = (first, first + 4)
    mine = n // 4

    def hello(device):
        pl.semaphore_signal(barrier, inc=1, device_id=device, device_id_type=MESH)

    def answer(i, device):
        pl.semaphore_signal(ready.at[i], inc=1, device_id=device, device_id_type=MESH)

    for device in (
        (c, n, right), (c, n, left), (c, n, across), (mate, n, t), (c_right, n, t), (c_left, n, t),
    ):
        hello(device)
    lower = jnp.where(n > 0, 1, 0) + jnp.where(n == 7, 1, 0)
    for other in others:
        lower = lower + jnp.where(other < n, 1, 0)

        @pl.when(other > n)
        def _():
            hello((c, other, t))

    @pl.when(n < 7)
    def _():
        hello(next_device)

    @pl.when(n == 0)
    def _():
        hello(before_device)

    pl.semaphore_wait(barrier, 6 + lower)
    for other in others:

        @pl.when(other < n)
        def _():
            answer(mine, (c, other, t))

    @pl.when(n > 0)
    def _():
        answer(2, before_device)

    @pl.when(n == 7)
    def _():
        answer(3, next_device)

    def emb_copy(k):
        other = first + 4 * k
        return copy(embed.at[other], emb.at[mine], S_EMB + k, S_EMB + mine, (c, other, t))

    for k, other in enumerate(others):

        @pl.when(other < n)
        def _():
            emb_copy(k).start()

        @pl.when(other == n)
        def _():
            pltpu.make_async_copy(embed.at[n], emb.at[mine], local.at[4]).start()

    own[0].wait()
    own[1].wait()
    to(enc_w.at[:, t, core], S_ENC_W, (c, n, right))
    to(enc_w.at[:, t, core], S_ENC_W + 1, (c, n, left))

    own[2].wait()
    own[3].wait()

    def kv_right(s):
        to(kv_w.at[:, lax.rem(y - s + 8, 8), core], S_KV_RIGHT + s, (c_right, n, t))

    def kv_left(s):
        to(kv_w.at[:, lax.rem(y + s, 8), core], S_KV_LEFT + s, (c_left, n, t))

    def kv_right_in(s):
        arrived(kv_w.at[:, lax.rem(y - s - 1 + 8, 8), core], S_KV_RIGHT + s)

    def kv_left_in(s):
        arrived(kv_w.at[:, lax.rem(y + s + 1, 8), core], S_KV_LEFT + s)

    def out_right(s):
        to(w_out.at[lax.rem(y - s + 8, 8), core], S_OUT_RIGHT + s, (c_right, n, t))

    def out_left(s):
        to(w_out.at[lax.rem(y + s, 8), core], S_OUT_LEFT + s, (c_left, n, t))

    def out_right_in(s):
        arrived(w_out.at[lax.rem(y - s - 1 + 8, 8), core], S_OUT_RIGHT + s)
        to(w_out.at[lax.rem(y - s - 1 + 8, 8), core], S_OUT_MATE + 1 + s, (mate, n, t))

    def out_left_in(s):
        arrived(w_out.at[lax.rem(y + s + 1, 8), core], S_OUT_LEFT + s)
        to(w_out.at[lax.rem(y + s + 1, 8), core], S_OUT_MATE + 5 + s, (mate, n, t))

    kv_right(0)
    kv_left(0)
    for k, other in enumerate(others):

        @pl.when(other > n)
        def _():
            pl.semaphore_wait(ready.at[k], 1)
            emb_copy(k).start()

    own[4].wait()
    own[5].wait()
    for st in range(4):
        at = slice(st * STRETCH_TOKENS, (st + 1) * STRETCH_TOKENS)
        packs[st] = jnp.concatenate([cond_k[:, at], cond_v[:, at]], axis=1)
    def pack_for(shard, k):
        return packs[slots[lax.rem(shard - n + 8, 4) + 4 * k, block] // 2]

    for side, device in enumerate((right, left)):
        for k in range(2):
            cond_send[side, k] = pack_for(device, k)
        cond_send[side, 2] = pack_for(across, side)
        to(cond_send.at[side], S_COND + side, (c, n, device), dst=cond_side.at[side])
    for k in range(2):
        cond_own[k] = pack_for(t, k)

    own[6].wait()

    @pl.when(n == 0)
    def _():
        pl.semaphore_wait(ready.at[3], 1)

    to(queries.at[pl.ds(0, STRETCH_TOKENS)], S_QUERY, before_device, dst=queries_next)
    own[8].wait()
    out_right(0)
    out_left(0)
    to(w_out.at[y, core], S_OUT_MATE, (mate, n, t))

    own[7].wait()
    row = lax.broadcasted_iota(jnp.int32, (8, 128), 0)
    count = jnp.zeros((8, 128), jnp.int32)
    for st in range(4):
        count = jnp.where(row // 2 == st, counts[st], count)
    mask = jnp.where((lax.rem(row, 2) < count) & (ids[...] != 0), 1.0, 0.0)
    for s in range(8):
        key_mask[s] = jnp.broadcast_to(mask[s : s + 1], (128, 128)).T

    kv_right_in(0)
    kv_right(1)
    kv_left_in(0)
    kv_left(1)
    arrived(enc_w.at[:, left, core], S_ENC_W)
    to(enc_w.at[0, left, core], S_ENC_W + 2, (c, n, right))
    to(enc_w.at[:, left, core], S_ENC_W + 4, (mate, n, t))
    arrived(enc_w.at[:, right, core], S_ENC_W + 1)
    to(enc_w.at[1, right, core], S_ENC_W + 3, (c, n, left))
    to(enc_w.at[:, right, core], S_ENC_W + 5, (mate, n, t))
    for side, device in enumerate((right, left)):
        arrived(cond_side.at[side], S_COND + side)
        to(cond_side.at[side, 2], (S_COND + 2, S_COND_LAST)[side], (c, n, device), dst=cond_across.at[side])
    kv_right_in(1)
    kv_right(2)
    kv_left_in(1)
    kv_left(2)

    for k in range(2):
        other = first + 4 * k

        @pl.when(other != n)
        def _():
            arrived(emb.at[k], S_EMB + k)

        @pl.when(other == n)
        def _():
            pltpu.make_async_copy(embed.at[n], emb.at[k], local.at[4]).wait()

        normed[k] = norm_rows(emb[k].astype(jnp.float32), gain_in[...].astype(jnp.float32).reshape(1, 768))

    def encode_heads(shard, states):
        query = dot(enc_w[0, shard].reshape(192, 768), normed[...].reshape(256, 768), NT)
        query = query.astype(jnp.bfloat16) * jnp.bfloat16(EHD ** (-0.5))
        columns = []
        for k in range(2):
            rows = []
            for h in range(3):
                at = slice(h * EHD, (h + 1) * EHD)
                both = states[k, at, :]
                scores = dot(both, query[at, k * 128 : (k + 1) * 128], TN)[:STRETCH_TOKENS]
                raised = jnp.exp(scores - jnp.max(scores, axis=0, keepdims=True))
                weights = (raised / jnp.sum(raised, axis=0, keepdims=True)).astype(jnp.bfloat16)
                spread = jnp.concatenate([jnp.zeros_like(weights), weights], axis=0)
                rows.append(dot(both, spread, NN).astype(jnp.bfloat16))
            columns.append(jnp.concatenate(rows, axis=0))
        mixed[shard] = jnp.concatenate(columns, axis=1)

    encode_heads(t, cond_own)
    arrived(enc_w.at[0, across, core], S_ENC_W + 2)
    to(enc_w.at[0, across, core], S_ENC_W + 6, (mate, n, t))
    arrived(enc_w.at[1, across, core], S_ENC_W + 3)
    to(enc_w.at[1, across, core], S_ENC_W + 7, (mate, n, t))
    out_right_in(0)
    out_right(1)
    out_left_in(0)
    out_left(1)
    arrived(enc_w.at[:, left, 1 - core], S_ENC_W + 4)
    encode_heads(left, cond_side.at[0])
    kv_right_in(2)
    kv_right(3)
    kv_left_in(2)
    arrived(enc_w.at[:, right, 1 - core], S_ENC_W + 5)
    encode_heads(right, cond_side.at[1])
    for side in range(2):
        arrived(cond_across.at[side], (S_COND + 2, S_COND_LAST)[side])
    arrived(enc_w.at[0, across, 1 - core], S_ENC_W + 6)
    encode_heads(across, cond_across)
    arrived(enc_w.at[1, across, 1 - core], S_ENC_W + 7)

    updated = dot(mixed[...].reshape(768, 256), enc_w[1].reshape(768, 768), TN)
    gain = gain_out[...].astype(jnp.float32).reshape(1, 768)
    for k in range(2):
        rows = emb[k].astype(jnp.float32) + updated[k * 128 : (k + 1) * 128]
        encoded[first + 4 * k] = norm_rows(rows, gain)

    for k in range(2):
        to(encoded.at[first + 4 * k], S_AG + 2 * k, (c, n, right))
        to(encoded.at[first + 4 * k], S_AG + 2 * k + 1, (c, n, left))

    kv_right_in(3)
    to(kv_w.at[:, :, core], S_KV_MATE, (mate, n, t))
    out_right_in(1)
    out_right(2)
    out_left_in(1)
    out_left(2)
    arrived(kv_w.at[:, :, 1 - core], S_KV_MATE)

    def project(rows):
        made = []
        for i in range(2):
            made.append(dot(rows, kv_w[i].reshape(768, 512), NN).astype(jnp.bfloat16))
        return made

    def project_pair(start):
        rows = jnp.concatenate([encoded[start], encoded[start + 4]], axis=0)
        got_k, got_v = project(rows)
        for k in range(2):
            keys[start + 4 * k] = got_k[k * 128 : (k + 1) * 128]
            values[start + 4 * k] = got_v[k * 128 : (k + 1) * 128]

    def first_of(shard):
        return lax.rem(shard - n + 8, 4)

    project_pair(first)
    arrived(encoded.at[first_of(left)], S_AG)
    to(encoded.at[first_of(left)], S_AG + 4, (c, n, right))
    arrived(encoded.at[first_of(right) + 4], S_AG + 3)
    to(encoded.at[first_of(right) + 4], S_AG + 5, (c, n, left))
    arrived(encoded.at[first_of(left) + 4], S_AG + 2)
    project_pair(first_of(left))
    arrived(encoded.at[first_of(right)], S_AG + 1)
    project_pair(first_of(right))
    out_right_in(2)
    out_right(3)
    out_left_in(2)
    arrived(encoded.at[first_of(across)], S_AG + 4)
    arrived(encoded.at[first_of(across) + 4], S_AG + 5)

    project_pair(first_of(across))

    slot_of = []
    for s in range(8):
        place = jnp.int32(0)
        for o in range(1, 8):
            place = jnp.where(slots[o, block] == s, o, place)
        slot_of.append(place)

    lane = lax.broadcasted_iota(jnp.int32, (1, 128), 1)
    use_lane = (lane >= STRETCH_TOKENS - 1) & (lane < 2 * STRETCH_TOKENS - 1)

    def attend(st, h, query_rows):
        at = slice(h * HEAD_WIDTH, (h + 1) * HEAD_WIDTH)
        pair = (slot_of[2 * st], slot_of[2 * st + 1])
        key_rows = jnp.concatenate([keys[p, :, at] for p in pair], axis=0)
        value_rows = jnp.concatenate([values[p, :, at] for p in pair], axis=0)
        allowed = key_mask[2 * st : 2 * st + 2].reshape(256, 128)
        scores = dot(key_rows, query_rows, NT) * HEAD_WIDTH ** (-0.5)
        scores = jnp.where(allowed > 0, scores, -1e30)
        raised = jnp.exp(scores - jnp.max(scores, axis=0, keepdims=True)) * allowed
        sums = jnp.sum(raised, axis=0, keepdims=True)
        use = (sums > 0) & use_lane
        share = jnp.where(use, 1.0 / jnp.where(use, sums, 1.0), 0.0)
        return dot((raised * share).astype(jnp.bfloat16), value_rows, TN)

    heads = [slice(h * HEAD_WIDTH, (h + 1) * HEAD_WIDTH) for h in range(4)]
    arrived(queries_next, S_QUERY)
    fourth = []
    for h, at in enumerate(heads):
        got = attend(3, h, jnp.concatenate([queries[192:256, at], queries_next[:, at]], axis=0))
        rows_send[:, at] = got[64:].astype(jnp.bfloat16)
        fourth.append(got[:64])

    @pl.when(n < 7)
    def _():
        pl.semaphore_wait(ready.at[2], 1)

    to(rows_send, S_PREV, next_device, dst=rows_got)

    def rows_of(shard, start, size):
        return attended.at[shard, pl.ds(start, size)]

    pieces = ((128, 128), (64, 64), (0, 64))

    def leave(i, rows):
        start, size = pieces[i]
        for h, at in enumerate(heads):
            attended[t, start : start + size, at] = rows[h].astype(jnp.bfloat16)
        to(rows_of(t, start, size), S_ATT + 4 * i, (c, n, right))
        to(rows_of(t, start, size), S_ATT + 4 * i + 1, (c, n, left))

    def pass_on(i):
        start, size = pieces[i]
        arrived(rows_of(left, start, size), S_ATT + 4 * i)
        to(rows_of(left, start, size // 2), S_ATT + 4 * i + 2, (c, n, right))
        arrived(rows_of(right, start, size), S_ATT + 4 * i + 1)
        to(rows_of(right, start + size // 2, size // 2), S_ATT + 4 * i + 3, (c, n, left))

    def passed_on(i):
        start, size = pieces[i]
        arrived(rows_of(across, start, size // 2), S_ATT + 4 * i + 2)
        arrived(rows_of(across, start + size // 2, size // 2), S_ATT + 4 * i + 3)

    got = [[attend(st, h, queries[64 * st : 64 * st + 128, at]) for h, at in enumerate(heads)] for st in (2, 1)]
    leave(
        0,
        [
            jnp.concatenate([got[1][h][64:] + got[0][h][:64], got[0][h][64:] + fourth[h]], axis=0)
            for h in range(4)
        ],
    )
    zero = [attend(0, h, queries[0:128, at]) for h, at in enumerate(heads)]
    leave(1, [zero[h][64:] + got[1][h][:64] for h in range(4)])
    arrived(rows_got, S_PREV)
    leave(2, [zero[h][:64] + jnp.where(block > 0, rows_got[:, at].astype(jnp.float32), 0.0) for h, at in enumerate(heads)])
    pass_on(0)
    pass_on(1)

    out_right_in(3)
    for i in range(8):
        at = y if i == 0 else (y - i + 8 if i < 5 else y + i - 4)
        arrived(w_out.at[lax.rem(at, 8), 1 - core], S_OUT_MATE + i)
    own[9].wait()

    def product(shard, rows=slice(0, 256)):
        return dot(attended[shard, rows], w_out[pl.ds(2 * shard, 2)].reshape(512, 1024), NN)

    total[...] = hidden[...].astype(jnp.float32) + product(t)
    pass_on(2)
    total[...] += product(left) + product(right)
    for i, rows in ((0, slice(128, 256)), (1, None), (2, slice(0, 128))):
        passed_on(i)
        if rows is not None:
            output[rows] = (total[rows] + product(across, rows)).astype(jnp.bfloat16)

    for k in range(2):

        @pl.when(first + 4 * k != n)
        def _():
            emb_copy(k).wait_send()

    for made in sent:
        made.wait_send()


def per_device(
    hidden,
    queries,
    key_weight_matrix,
    value_weight_matrix,
    w_out,
    neighbour_embed,
    neighbour_ids,
    neighbour_count,
    slot_seq,
    cond_keys,
    cond_values,
    enc_gain,
    enc_query,
    enc_out,
    final_gain,
):
    vmem, hbm = pl.BlockSpec(memory_space=pltpu.VMEM), pl.BlockSpec(memory_space=pltpu.HBM)
    smem = pl.BlockSpec(memory_space=pltpu.SMEM)
    bf16, f32 = jnp.bfloat16, jnp.float32
    return pl.pallas_call(
        body,
        out_shape=jax.ShapeDtypeStruct((256, 1024), bf16),
        in_specs=[smem, smem, *[hbm] * 11, vmem, vmem],
        out_specs=vmem,
        scratch_shapes=[
            pltpu.VMEM((192, 256), bf16),
            pltpu.VMEM((192, 256), bf16),
            pltpu.VMEM((256, 512), bf16),
            pltpu.VMEM((8, 128), jnp.int32),
            pltpu.VMEM((8, 2, 128, 1024), bf16),
            pltpu.VMEM((256, 1024), bf16),
            pltpu.VMEM((256, 1024), f32),
            pltpu.VMEM((4, 256, 512), bf16),
            pltpu.VMEM((64, 512), bf16),
            pltpu.VMEM((64, 512), bf16),
            pltpu.VMEM((64, 512), bf16),
            pltpu.VMEM((2, 128, 768), bf16),
            pltpu.VMEM((4, 192, 128), bf16),
            pltpu.VMEM((2, 3, 192, 128), bf16),
            pltpu.VMEM((2, 192, 128), bf16),
            pltpu.VMEM((2, 3, 192, 128), bf16),
            pltpu.VMEM((2, 192, 128), bf16),
            pltpu.VMEM((2, 4, 2, 96, 768), bf16),
            pltpu.VMEM((2, 128, 768), bf16),
            pltpu.VMEM((4, 192, 256), bf16),
            pltpu.VMEM((8, 128, 768), bf16),
            pltpu.VMEM((2, 8, 2, 48, 512), bf16),
            pltpu.VMEM((8, 128, 512), bf16),
            pltpu.VMEM((8, 128, 512), bf16),
            pltpu.VMEM((8, 128, 128), f32),
            pltpu.SemaphoreType.DMA((N_SEMS,)),
            pltpu.SemaphoreType.DMA((N_SEMS,)),
            pltpu.SemaphoreType.DMA((11,)),
            pltpu.SemaphoreType.REGULAR((4,)),
        ],
        compiler_params=pltpu.CompilerParams(
            collective_id=0, has_side_effects=True, vmem_limit_bytes=62 * 2**20
        ),
        cost_estimate=pl.CostEstimate(flops=4 * 10**9, bytes_accessed=150 * 10**6, transcendentals=0),
    )(
        slot_seq.T,
        neighbour_count,
        neighbour_embed,
        cond_keys.T,
        cond_values.T,
        enc_query.T.reshape(2, 96, 768),
        enc_out.reshape(2, 96, 768),
        key_weight_matrix,
        value_weight_matrix,
        queries,
        neighbour_ids,
        w_out,
        hidden,
        enc_gain,
        final_gain,
    )


def solution(mesh):
    in_specs = (
        P(("ctx", "nbr"), "tp"),
        P(("ctx", "nbr"), "tp"),
        P("ctx", "tp"),
        P("ctx", "tp"),
        P("ctx", "tp"),
        P(("ctx", "nbr"), None, None),
        P(("ctx", "nbr"), None),
        P(("ctx", "nbr")),
        P(),
        P(("ctx", "nbr"), "tp"),
        P(("ctx", "nbr"), "tp"),
        P(),
        P(None, "tp"),
        P("tp", None),
        P(),
    )
    out_specs = P(("ctx", "nbr"), "tp")
    return jax.shard_map(
        per_device, mesh=mesh, in_specs=in_specs, out_specs=out_specs, check_vma=False
    )
```

```python
import jax
import jax.numpy as jnp
from jax import lax
from jax.experimental import pallas as pl
from jax.experimental.pallas import tpu as pltpu
from jax.sharding import PartitionSpec as P

HEAD_WIDTH = 128
EHD = 64
STRETCH_TOKENS = 64
NEIGHBOUR_TOKENS = 128
EPSILON = 1e-06
MESH = pl.DeviceIdType.MESH
NT = (((1,), (1,)), ((), ()))
TN = (((0,), (0,)), ((), ()))
NN = (((1,), (0,)), ((), ()))

S_EMB, S_COND, S_ENC_W, S_KV_RIGHT, S_KV_LEFT, S_KV_MATE, S_QUERY, S_AG, S_PREV, S_ATT = (
    0, 2, 5, 13, 17, 20, 21, 22, 28, 29,
)
S_OUT_RIGHT, S_OUT_LEFT, S_OUT_MATE = 41, 45, 48
S_COND_LAST = 56
N_SEMS = 57


def dot(a, b, dims):
    return lax.dot_general(a, b, dims, preferred_element_type=jnp.float32)


def norm_rows(rows, gain):
    scale = lax.rsqrt(jnp.mean(rows * rows, axis=-1, keepdims=True) + EPSILON)
    return (rows * scale * gain).astype(jnp.bfloat16)


def body(
    slots, counts, embed, cond_k_far, cond_v_far, enc_q, enc_o, key_w, value_w, queries_far, ids_far, w_far, hidden_far,
    gain_in, gain_out,
    output,
    cond_k, cond_v, queries, ids, w_out, hidden, total, attended, queries_next, rows_send, rows_got,
    emb, packs, cond_send, cond_own, cond_side, cond_across, enc_w, normed, mixed, encoded, kv_w, keys, values, key_mask, send, recv, local, ready,
):
    c, n, t = lax.axis_index("ctx"), lax.axis_index("nbr"), lax.axis_index("tp")
    block = c * 8 + n
    right, left, across = lax.rem(t + 1, 4), lax.rem(t + 3, 4), lax.rem(t + 2, 4)
    core = lax.rem(c, 2)
    y = c // 2
    mate = c + 1 - 2 * core
    c_right, c_left = lax.rem(c + 2, 16), lax.rem(c + 14, 16)
    first = lax.rem(t - n + 8, 4)
    nxt = lax.rem(block + 1, 128)
    before = lax.rem(block + 127, 128)
    next_device = (nxt // 8, lax.rem(nxt, 8), t)
    before_device = (before // 8, lax.rem(before, 8), t)

    def copy(src, dst, s, r, device):
        return pltpu.make_async_remote_copy(
            src_ref=src, dst_ref=dst, send_sem=send.at[s], recv_sem=recv.at[r],
            device_id=device, device_id_type=MESH,
        )

    def to(ref, s, device, dst=None, r=None):
        made = copy(ref, ref if dst is None else dst, s, s if r is None else r, device)
        made.start()
        sent.append(made)

    def arrived(ref, r):
        copy(ref, ref, r, r, (c, n, right)).wait_recv()

    sent = []

    own = [
        pltpu.make_async_copy(enc_q, enc_w.at[0, t], local.at[0]),
        pltpu.make_async_copy(enc_o, enc_w.at[1, t], local.at[1]),
        pltpu.make_async_copy(key_w, kv_w.at[0, y, core], local.at[2]),
        pltpu.make_async_copy(value_w, kv_w.at[1, y, core], local.at[3]),
        pltpu.make_async_copy(cond_k_far, cond_k, local.at[5]),
        pltpu.make_async_copy(cond_v_far, cond_v, local.at[6]),
        pltpu.make_async_copy(queries_far, queries, local.at[7]),
        pltpu.make_async_copy(ids_far, ids, local.at[8]),
        pltpu.make_async_copy(w_far, w_out.at[y, core], local.at[9]),
        pltpu.make_async_copy(hidden_far, hidden, local.at[10]),
    ]
    for made in own:
        made.start()

    barrier = pltpu.get_barrier_semaphore()
    others = (first, first + 4)
    mine = n // 4

    def hello(device):
        pl.semaphore_signal(barrier, inc=1, device_id=device, device_id_type=MESH)

    def answer(i, device):
        pl.semaphore_signal(ready.at[i], inc=1, device_id=device, device_id_type=MESH)

    for device in (
        (c, n, right), (c, n, left), (c, n, across), (mate, n, t), (c_right, n, t), (c_left, n, t),
    ):
        hello(device)
    lower = jnp.where(n > 0, 1, 0) + jnp.where(n == 7, 1, 0)
    for other in others:
        lower = lower + jnp.where(other < n, 1, 0)

        @pl.when(other > n)
        def _():
            hello((c, other, t))

    @pl.when(n < 7)
    def _():
        hello(next_device)

    @pl.when(n == 0)
    def _():
        hello(before_device)

    pl.semaphore_wait(barrier, 6 + lower)
    for other in others:

        @pl.when(other < n)
        def _():
            answer(mine, (c, other, t))

    @pl.when(n > 0)
    def _():
        answer(2, before_device)

    @pl.when(n == 7)
    def _():
        answer(3, next_device)

    def emb_copy(k):
        other = first + 4 * k
        return copy(embed.at[other], emb.at[mine], S_EMB + k, S_EMB + mine, (c, other, t))

    for k, other in enumerate(others):

        @pl.when(other < n)
        def _():
            emb_copy(k).start()

        @pl.when(other == n)
        def _():
            pltpu.make_async_copy(embed.at[n], emb.at[mine], local.at[4]).start()

    own[0].wait()
    own[1].wait()
    to(enc_w.at[:, t, core], S_ENC_W, (c, n, right))
    to(enc_w.at[:, t, core], S_ENC_W + 1, (c, n, left))

    own[2].wait()
    own[3].wait()

    def kv_right(s):
        to(kv_w.at[:, lax.rem(y - s + 8, 8), core], S_KV_RIGHT + s, (c_right, n, t))

    def kv_left(s):
        to(kv_w.at[:, lax.rem(y + s, 8), core], S_KV_LEFT + s, (c_left, n, t))

    def kv_right_in(s):
        arrived(kv_w.at[:, lax.rem(y - s - 1 + 8, 8), core], S_KV_RIGHT + s)

    def kv_left_in(s):
        arrived(kv_w.at[:, lax.rem(y + s + 1, 8), core], S_KV_LEFT + s)

    def out_right(s):
        to(w_out.at[lax.rem(y - s + 8, 8), core], S_OUT_RIGHT + s, (c_right, n, t))

    def out_left(s):
        to(w_out.at[lax.rem(y + s, 8), core], S_OUT_LEFT + s, (c_left, n, t))

    def out_right_in(s):
        arrived(w_out.at[lax.rem(y - s - 1 + 8, 8), core], S_OUT_RIGHT + s)
        to(w_out.at[lax.rem(y - s - 1 + 8, 8), core], S_OUT_MATE + 1 + s, (mate, n, t))

    def out_left_in(s):
        arrived(w_out.at[lax.rem(y + s + 1, 8), core], S_OUT_LEFT + s)
        to(w_out.at[lax.rem(y + s + 1, 8), core], S_OUT_MATE + 5 + s, (mate, n, t))

    kv_right(0)
    kv_left(0)
    for k, other in enumerate(others):

        @pl.when(other > n)
        def _():
            pl.semaphore_wait(ready.at[k], 1)
            emb_copy(k).start()

    own[4].wait()
    own[5].wait()
    for st in range(4):
        at = slice(st * STRETCH_TOKENS, (st + 1) * STRETCH_TOKENS)
        packs[st] = jnp.concatenate([cond_k[:, at], cond_v[:, at]], axis=1)
    def pack_for(shard, k):
        return packs[slots[lax.rem(shard - n + 8, 4) + 4 * k, block] // 2]

    for side, device in enumerate((right, left)):
        for k in range(2):
            cond_send[side, k] = pack_for(device, k)
        cond_send[side, 2] = pack_for(across, side)
        to(cond_send.at[side], S_COND + side, (c, n, device), dst=cond_side.at[side])
    for k in range(2):
        cond_own[k] = pack_for(t, k)

    own[6].wait()

    @pl.when(n == 0)
    def _():
        pl.semaphore_wait(ready.at[3], 1)

    to(queries.at[pl.ds(0, STRETCH_TOKENS)], S_QUERY, before_device, dst=queries_next)
    own[8].wait()
    out_right(0)
    out_left(0)
    to(w_out.at[y, core], S_OUT_MATE, (mate, n, t))

    own[7].wait()
    row = lax.broadcasted_iota(jnp.int32, (8, 128), 0)
    count = jnp.zeros((8, 128), jnp.int32)
    for st in range(4):
        count = jnp.where(row // 2 == st, counts[st], count)
    mask = jnp.where((lax.rem(row, 2) < count) & (ids[...] != 0), 1.0, 0.0)
    for s in range(8):
        key_mask[s] = jnp.broadcast_to(mask[s : s + 1], (128, 128)).T

    kv_right_in(0)
    kv_right(1)
    kv_left_in(0)
    kv_left(1)
    arrived(enc_w.at[:, left, core], S_ENC_W)
    to(enc_w.at[0, left, core], S_ENC_W + 2, (c, n, right))
    to(enc_w.at[:, left, core], S_ENC_W + 4, (mate, n, t))
    arrived(enc_w.at[:, right, core], S_ENC_W + 1)
    to(enc_w.at[1, right, core], S_ENC_W + 3, (c, n, left))
    to(enc_w.at[:, right, core], S_ENC_W + 5, (mate, n, t))
    for side, device in enumerate((right, left)):
        arrived(cond_side.at[side], S_COND + side)
        to(cond_side.at[side, 2], (S_COND + 2, S_COND_LAST)[side], (c, n, device), dst=cond_across.at[side])
    kv_right_in(1)
    kv_right(2)
    kv_left_in(1)
    kv_left(2)

    def take(k):
        other = others[k]

        @pl.when(other != n)
        def _():
            arrived(emb.at[k], S_EMB + k)

        @pl.when(other == n)
        def _():
            pltpu.make_async_copy(embed.at[n], emb.at[k], local.at[4]).wait()

        normed[k] = norm_rows(emb[k].astype(jnp.float32), gain_in[...].astype(jnp.float32).reshape(1, 768))

    def encode_heads(shard, states, k):
        query = dot(enc_w[0, shard].reshape(192, 768), normed[k], NT)
        query = query.astype(jnp.bfloat16) * jnp.bfloat16(EHD ** (-0.5))
        rows = []
        for h in range(3):
            at = slice(h * EHD, (h + 1) * EHD)
            both = states[k, at, :]
            scores = dot(both, query[at], TN)[:STRETCH_TOKENS]
            raised = jnp.exp(scores - jnp.max(scores, axis=0, keepdims=True))
            weights = (raised / jnp.sum(raised, axis=0, keepdims=True)).astype(jnp.bfloat16)
            spread = jnp.concatenate([jnp.zeros_like(weights), weights], axis=0)
            rows.append(dot(both, spread, NN).astype(jnp.bfloat16))
        mixed[k, shard] = jnp.concatenate(rows, axis=0)

    def finish(k):
        updated = dot(mixed[k].reshape(768, 128), enc_w[1].reshape(768, 768), TN)
        rows = emb[k].astype(jnp.float32) + updated
        encoded[first + 4 * k] = norm_rows(rows, gain_out[...].astype(jnp.float32).reshape(1, 768))
        to(encoded.at[first + 4 * k], S_AG + 2 * k, (c, n, right))
        to(encoded.at[first + 4 * k], S_AG + 2 * k + 1, (c, n, left))

    take(0)
    encode_heads(t, cond_own, 0)
    arrived(enc_w.at[0, across, core], S_ENC_W + 2)
    to(enc_w.at[0, across, core], S_ENC_W + 6, (mate, n, t))
    arrived(enc_w.at[1, across, core], S_ENC_W + 3)
    to(enc_w.at[1, across, core], S_ENC_W + 7, (mate, n, t))
    out_right_in(0)
    out_right(1)
    out_left_in(0)
    out_left(1)
    arrived(enc_w.at[:, left, 1 - core], S_ENC_W + 4)
    encode_heads(left, cond_side.at[0], 0)
    kv_right_in(2)
    kv_right(3)
    kv_left_in(2)
    arrived(enc_w.at[:, right, 1 - core], S_ENC_W + 5)
    encode_heads(right, cond_side.at[1], 0)
    for side in range(2):
        arrived(cond_across.at[side], (S_COND + 2, S_COND_LAST)[side])
    arrived(enc_w.at[0, across, 1 - core], S_ENC_W + 6)
    encode_heads(across, cond_across, 0)
    arrived(enc_w.at[1, across, 1 - core], S_ENC_W + 7)

    finish(0)
    take(1)
    for shard, states in ((t, cond_own), (left, cond_side.at[0]), (right, cond_side.at[1]), (across, cond_across)):
        encode_heads(shard, states, 1)
    finish(1)

    kv_right_in(3)
    to(kv_w.at[:, :, core], S_KV_MATE, (mate, n, t))
    out_right_in(1)
    out_right(2)
    out_left_in(1)
    out_left(2)
    arrived(kv_w.at[:, :, 1 - core], S_KV_MATE)

    def project(rows):
        made = []
        for i in range(2):
            made.append(dot(rows, kv_w[i].reshape(768, 512), NN).astype(jnp.bfloat16))
        return made

    def project_pair(start):
        rows = jnp.concatenate([encoded[start], encoded[start + 4]], axis=0)
        got_k, got_v = project(rows)
        for k in range(2):
            keys[start + 4 * k] = got_k[k * 128 : (k + 1) * 128]
            values[start + 4 * k] = got_v[k * 128 : (k + 1) * 128]

    def first_of(shard):
        return lax.rem(shard - n + 8, 4)

    project_pair(first)
    arrived(encoded.at[first_of(left)], S_AG)
    to(encoded.at[first_of(left)], S_AG + 4, (c, n, right))
    arrived(encoded.at[first_of(right) + 4], S_AG + 3)
    to(encoded.at[first_of(right) + 4], S_AG + 5, (c, n, left))
    arrived(encoded.at[first_of(left) + 4], S_AG + 2)
    project_pair(first_of(left))
    arrived(encoded.at[first_of(right)], S_AG + 1)
    project_pair(first_of(right))
    out_right_in(2)
    out_right(3)
    out_left_in(2)
    arrived(encoded.at[first_of(across)], S_AG + 4)
    arrived(encoded.at[first_of(across) + 4], S_AG + 5)

    project_pair(first_of(across))

    slot_of = []
    for s in range(8):
        place = jnp.int32(0)
        for o in range(1, 8):
            place = jnp.where(slots[o, block] == s, o, place)
        slot_of.append(place)

    lane = lax.broadcasted_iota(jnp.int32, (1, 128), 1)
    use_lane = (lane >= STRETCH_TOKENS - 1) & (lane < 2 * STRETCH_TOKENS - 1)

    def attend(st, h, query_rows):
        at = slice(h * HEAD_WIDTH, (h + 1) * HEAD_WIDTH)
        pair = (slot_of[2 * st], slot_of[2 * st + 1])
        key_rows = jnp.concatenate([keys[p, :, at] for p in pair], axis=0)
        value_rows = jnp.concatenate([values[p, :, at] for p in pair], axis=0)
        allowed = key_mask[2 * st : 2 * st + 2].reshape(256, 128)
        scores = dot(key_rows, query_rows, NT) * HEAD_WIDTH ** (-0.5)
        scores = jnp.where(allowed > 0, scores, -1e30)
        raised = jnp.exp(scores - jnp.max(scores, axis=0, keepdims=True)) * allowed
        sums = jnp.sum(raised, axis=0, keepdims=True)
        use = (sums > 0) & use_lane
        share = jnp.where(use, 1.0 / jnp.where(use, sums, 1.0), 0.0)
        return dot((raised * share).astype(jnp.bfloat16), value_rows, TN)

    heads = [slice(h * HEAD_WIDTH, (h + 1) * HEAD_WIDTH) for h in range(4)]
    arrived(queries_next, S_QUERY)
    fourth = []
    for h, at in enumerate(heads):
        got = attend(3, h, jnp.concatenate([queries[192:256, at], queries_next[:, at]], axis=0))
        rows_send[:, at] = got[64:].astype(jnp.bfloat16)
        fourth.append(got[:64])

    @pl.when(n < 7)
    def _():
        pl.semaphore_wait(ready.at[2], 1)

    to(rows_send, S_PREV, next_device, dst=rows_got)

    def rows_of(shard, start, size):
        return attended.at[shard, pl.ds(start, size)]

    pieces = ((128, 128), (64, 64), (0, 64))

    def leave(i, rows):
        start, size = pieces[i]
        for h, at in enumerate(heads):
            attended[t, start : start + size, at] = rows[h].astype(jnp.bfloat16)
        to(rows_of(t, start, size), S_ATT + 4 * i, (c, n, right))
        to(rows_of(t, start, size), S_ATT + 4 * i + 1, (c, n, left))

    def pass_on(i):
        start, size = pieces[i]
        arrived(rows_of(left, start, size), S_ATT + 4 * i)
        to(rows_of(left, start, size // 2), S_ATT + 4 * i + 2, (c, n, right))
        arrived(rows_of(right, start, size), S_ATT + 4 * i + 1)
        to(rows_of(right, start + size // 2, size // 2), S_ATT + 4 * i + 3, (c, n, left))

    def passed_on(i):
        start, size = pieces[i]
        arrived(rows_of(across, start, size // 2), S_ATT + 4 * i + 2)
        arrived(rows_of(across, start + size // 2, size // 2), S_ATT + 4 * i + 3)

    got = [[attend(st, h, queries[64 * st : 64 * st + 128, at]) for h, at in enumerate(heads)] for st in (2, 1)]
    leave(
        0,
        [
            jnp.concatenate([got[1][h][64:] + got[0][h][:64], got[0][h][64:] + fourth[h]], axis=0)
            for h in range(4)
        ],
    )
    zero = [attend(0, h, queries[0:128, at]) for h, at in enumerate(heads)]
    leave(1, [zero[h][64:] + got[1][h][:64] for h in range(4)])
    arrived(rows_got, S_PREV)
    leave(2, [zero[h][:64] + jnp.where(block > 0, rows_got[:, at].astype(jnp.float32), 0.0) for h, at in enumerate(heads)])
    pass_on(0)
    pass_on(1)

    out_right_in(3)
    for i in range(8):
        at = y if i == 0 else (y - i + 8 if i < 5 else y + i - 4)
        arrived(w_out.at[lax.rem(at, 8), 1 - core], S_OUT_MATE + i)
    own[9].wait()

    def product(shard, rows=slice(0, 256)):
        return dot(attended[shard, rows], w_out[pl.ds(2 * shard, 2)].reshape(512, 1024), NN)

    total[...] = hidden[...].astype(jnp.float32) + product(t)
    pass_on(2)
    total[...] += product(left) + product(right)
    for i, rows in ((0, slice(128, 256)), (1, None), (2, slice(0, 128))):
        passed_on(i)
        if rows is not None:
            output[rows] = (total[rows] + product(across, rows)).astype(jnp.bfloat16)

    for k in range(2):

        @pl.when(first + 4 * k != n)
        def _():
            emb_copy(k).wait_send()

    for made in sent:
        made.wait_send()


def per_device(
    hidden,
    queries,
    key_weight_matrix,
    value_weight_matrix,
    w_out,
    neighbour_embed,
    neighbour_ids,
    neighbour_count,
    slot_seq,
    cond_keys,
    cond_values,
    enc_gain,
    enc_query,
    enc_out,
    final_gain,
):
    vmem, hbm = pl.BlockSpec(memory_space=pltpu.VMEM), pl.BlockSpec(memory_space=pltpu.HBM)
    smem = pl.BlockSpec(memory_space=pltpu.SMEM)
    bf16, f32 = jnp.bfloat16, jnp.float32
    return pl.pallas_call(
        body,
        out_shape=jax.ShapeDtypeStruct((256, 1024), bf16),
        in_specs=[smem, smem, *[hbm] * 11, vmem, vmem],
        out_specs=vmem,
        scratch_shapes=[
            pltpu.VMEM((192, 256), bf16),
            pltpu.VMEM((192, 256), bf16),
            pltpu.VMEM((256, 512), bf16),
            pltpu.VMEM((8, 128), jnp.int32),
            pltpu.VMEM((8, 2, 128, 1024), bf16),
            pltpu.VMEM((256, 1024), bf16),
            pltpu.VMEM((256, 1024), f32),
            pltpu.VMEM((4, 256, 512), bf16),
            pltpu.VMEM((64, 512), bf16),
            pltpu.VMEM((64, 512), bf16),
            pltpu.VMEM((64, 512), bf16),
            pltpu.VMEM((2, 128, 768), bf16),
            pltpu.VMEM((4, 192, 128), bf16),
            pltpu.VMEM((2, 3, 192, 128), bf16),
            pltpu.VMEM((2, 192, 128), bf16),
            pltpu.VMEM((2, 3, 192, 128), bf16),
            pltpu.VMEM((2, 192, 128), bf16),
            pltpu.VMEM((2, 4, 2, 96, 768), bf16),
            pltpu.VMEM((2, 128, 768), bf16),
            pltpu.VMEM((2, 4, 192, 128), bf16),
            pltpu.VMEM((8, 128, 768), bf16),
            pltpu.VMEM((2, 8, 2, 48, 512), bf16),
            pltpu.VMEM((8, 128, 512), bf16),
            pltpu.VMEM((8, 128, 512), bf16),
            pltpu.VMEM((8, 128, 128), f32),
            pltpu.SemaphoreType.DMA((N_SEMS,)),
            pltpu.SemaphoreType.DMA((N_SEMS,)),
            pltpu.SemaphoreType.DMA((11,)),
            pltpu.SemaphoreType.REGULAR((4,)),
        ],
        compiler_params=pltpu.CompilerParams(
            collective_id=0, has_side_effects=True, vmem_limit_bytes=62 * 2**20
        ),
        cost_estimate=pl.CostEstimate(flops=4 * 10**9, bytes_accessed=150 * 10**6, transcendentals=0),
    )(
        slot_seq.T,
        neighbour_count,
        neighbour_embed,
        cond_keys.T,
        cond_values.T,
        enc_query.T.reshape(2, 96, 768),
        enc_out.reshape(2, 96, 768),
        key_weight_matrix,
        value_weight_matrix,
        queries,
        neighbour_ids,
        w_out,
        hidden,
        enc_gain,
        final_gain,
    )


def solution(mesh):
    in_specs = (
        P(("ctx", "nbr"), "tp"),
        P(("ctx", "nbr"), "tp"),
        P("ctx", "tp"),
        P("ctx", "tp"),
        P("ctx", "tp"),
        P(("ctx", "nbr"), None, None),
        P(("ctx", "nbr"), None),
        P(("ctx", "nbr")),
        P(),
        P(("ctx", "nbr"), "tp"),
        P(("ctx", "nbr"), "tp"),
        P(),
        P(None, "tp"),
        P("tp", None),
        P(),
    )
    out_specs = P(("ctx", "nbr"), "tp")
    return jax.shard_map(
        per_device, mesh=mesh, in_specs=in_specs, out_specs=out_specs, check_vma=False
    )
```

```python
import jax
import jax.numpy as jnp
from jax import lax
from jax.experimental import pallas as pl
from jax.experimental.pallas import tpu as pltpu
from jax.sharding import PartitionSpec as P

HEAD_WIDTH = 128
EHD = 64
STRETCH_TOKENS = 64
NEIGHBOUR_TOKENS = 128
EPSILON = 1e-06
MESH = pl.DeviceIdType.MESH
NT = (((1,), (1,)), ((), ()))
TN = (((0,), (0,)), ((), ()))
NN = (((1,), (0,)), ((), ()))

S_EMB, S_COND, S_ENC_W, S_KV_RIGHT, S_KV_LEFT, S_KV_MATE, S_QUERY, S_AG, S_PREV, S_ATT = (
    0, 2, 5, 13, 17, 20, 21, 22, 28, 29,
)
S_OUT_RIGHT, S_OUT_LEFT, S_OUT_MATE = 41, 45, 48
S_COND_LAST, S_AG_ON = 56, 57
N_SEMS = 61


def dot(a, b, dims):
    return lax.dot_general(a, b, dims, preferred_element_type=jnp.float32)


def norm_rows(rows, gain):
    scale = lax.rsqrt(jnp.mean(rows * rows, axis=-1, keepdims=True) + EPSILON)
    return (rows * scale * gain).astype(jnp.bfloat16)


def body(
    slots, counts, embed, cond_k_far, cond_v_far, enc_q, enc_o, key_w, value_w, queries_far, ids_far, w_far, hidden_far,
    gain_in, gain_out,
    output,
    cond_k, cond_v, queries, ids, w_out, hidden, total, attended, queries_next, rows_send, rows_got,
    emb, packs, cond_send, cond_own, cond_side, cond_across, enc_w, normed, mixed, encoded, kv_w, keys, values, key_mask, send, recv, local, ready,
):
    c, n, t = lax.axis_index("ctx"), lax.axis_index("nbr"), lax.axis_index("tp")
    block = c * 8 + n
    right, left, across = lax.rem(t + 1, 4), lax.rem(t + 3, 4), lax.rem(t + 2, 4)
    core = lax.rem(c, 2)
    y = c // 2
    mate = c + 1 - 2 * core
    c_right, c_left = lax.rem(c + 2, 16), lax.rem(c + 14, 16)
    first = lax.rem(t - n + 8, 4)
    nxt = lax.rem(block + 1, 128)
    before = lax.rem(block + 127, 128)
    next_device = (nxt // 8, lax.rem(nxt, 8), t)
    before_device = (before // 8, lax.rem(before, 8), t)

    def copy(src, dst, s, r, device):
        return pltpu.make_async_remote_copy(
            src_ref=src, dst_ref=dst, send_sem=send.at[s], recv_sem=recv.at[r],
            device_id=device, device_id_type=MESH,
        )

    def to(ref, s, device, dst=None, r=None):
        made = copy(ref, ref if dst is None else dst, s, s if r is None else r, device)
        made.start()
        sent.append(made)

    def arrived(ref, r):
        copy(ref, ref, r, r, (c, n, right)).wait_recv()

    sent = []

    own = [
        pltpu.make_async_copy(enc_q, enc_w.at[0, t], local.at[0]),
        pltpu.make_async_copy(enc_o, enc_w.at[1, t], local.at[1]),
        pltpu.make_async_copy(key_w, kv_w.at[0, y, core], local.at[2]),
        pltpu.make_async_copy(value_w, kv_w.at[1, y, core], local.at[3]),
        pltpu.make_async_copy(cond_k_far, cond_k, local.at[5]),
        pltpu.make_async_copy(cond_v_far, cond_v, local.at[6]),
        pltpu.make_async_copy(queries_far, queries, local.at[7]),
        pltpu.make_async_copy(ids_far, ids, local.at[8]),
        pltpu.make_async_copy(w_far, w_out.at[y, core], local.at[9]),
        pltpu.make_async_copy(hidden_far, hidden, local.at[10]),
    ]
    for made in own:
        made.start()

    barrier = pltpu.get_barrier_semaphore()
    others = (first, first + 4)
    mine = n // 4

    def hello(device):
        pl.semaphore_signal(barrier, inc=1, device_id=device, device_id_type=MESH)

    def answer(i, device):
        pl.semaphore_signal(ready.at[i], inc=1, device_id=device, device_id_type=MESH)

    for device in (
        (c, n, right), (c, n, left), (c, n, across), (mate, n, t), (c_right, n, t), (c_left, n, t),
    ):
        hello(device)
    lower = jnp.where(n > 0, 1, 0) + jnp.where(n == 7, 1, 0)
    for other in others:
        lower = lower + jnp.where(other < n, 1, 0)

        @pl.when(other > n)
        def _():
            hello((c, other, t))

    @pl.when(n < 7)
    def _():
        hello(next_device)

    @pl.when(n == 0)
    def _():
        hello(before_device)

    pl.semaphore_wait(barrier, 6 + lower)
    for other in others:

        @pl.when(other < n)
        def _():
            answer(mine, (c, other, t))

    @pl.when(n > 0)
    def _():
        answer(2, before_device)

    @pl.when(n == 7)
    def _():
        answer(3, next_device)

    def emb_copy(k):
        other = first + 4 * k
        return copy(embed.at[other], emb.at[mine], S_EMB + k, S_EMB + mine, (c, other, t))

    for k, other in enumerate(others):

        @pl.when(other < n)
        def _():
            emb_copy(k).start()

        @pl.when(other == n)
        def _():
            pltpu.make_async_copy(embed.at[n], emb.at[mine], local.at[4]).start()

    own[0].wait()
    own[1].wait()
    to(enc_w.at[:, t, core], S_ENC_W, (c, n, right))
    to(enc_w.at[:, t, core], S_ENC_W + 1, (c, n, left))

    own[2].wait()
    own[3].wait()

    def kv_right(s):
        to(kv_w.at[:, lax.rem(y - s + 8, 8), core], S_KV_RIGHT + s, (c_right, n, t))

    def kv_left(s):
        to(kv_w.at[:, lax.rem(y + s, 8), core], S_KV_LEFT + s, (c_left, n, t))

    def kv_right_in(s):
        arrived(kv_w.at[:, lax.rem(y - s - 1 + 8, 8), core], S_KV_RIGHT + s)

    def kv_left_in(s):
        arrived(kv_w.at[:, lax.rem(y + s + 1, 8), core], S_KV_LEFT + s)

    def out_right(s):
        to(w_out.at[lax.rem(y - s + 8, 8), core], S_OUT_RIGHT + s, (c_right, n, t))

    def out_left(s):
        to(w_out.at[lax.rem(y + s, 8), core], S_OUT_LEFT + s, (c_left, n, t))

    def out_right_in(s):
        arrived(w_out.at[lax.rem(y - s - 1 + 8, 8), core], S_OUT_RIGHT + s)
        to(w_out.at[lax.rem(y - s - 1 + 8, 8), core], S_OUT_MATE + 1 + s, (mate, n, t))

    def out_left_in(s):
        arrived(w_out.at[lax.rem(y + s + 1, 8), core], S_OUT_LEFT + s)
        to(w_out.at[lax.rem(y + s + 1, 8), core], S_OUT_MATE + 5 + s, (mate, n, t))

    kv_right(0)
    kv_left(0)
    for k, other in enumerate(others):

        @pl.when(other > n)
        def _():
            pl.semaphore_wait(ready.at[k], 1)
            emb_copy(k).start()

    own[4].wait()
    own[5].wait()
    for st in range(4):
        at = slice(st * STRETCH_TOKENS, (st + 1) * STRETCH_TOKENS)
        packs[st] = jnp.concatenate([cond_k[:, at], cond_v[:, at]], axis=1)
    def pack_for(shard, k):
        return packs[slots[lax.rem(shard - n + 8, 4) + 4 * k, block] // 2]

    for side, device in enumerate((right, left)):
        for k in range(2):
            cond_send[side, k] = pack_for(device, k)
        cond_send[side, 2] = pack_for(across, side)
        to(cond_send.at[side], S_COND + side, (c, n, device), dst=cond_side.at[side])
    for k in range(2):
        cond_own[k] = pack_for(t, k)

    own[6].wait()

    @pl.when(n == 0)
    def _():
        pl.semaphore_wait(ready.at[3], 1)

    to(queries.at[pl.ds(0, STRETCH_TOKENS)], S_QUERY, before_device, dst=queries_next)
    own[8].wait()
    out_right(0)
    out_left(0)
    to(w_out.at[y, core], S_OUT_MATE, (mate, n, t))

    own[7].wait()
    row = lax.broadcasted_iota(jnp.int32, (8, 128), 0)
    count = jnp.zeros((8, 128), jnp.int32)
    for st in range(4):
        count = jnp.where(row // 2 == st, counts[st], count)
    mask = jnp.where((lax.rem(row, 2) < count) & (ids[...] != 0), 1.0, 0.0)
    for s in range(8):
        key_mask[s] = jnp.broadcast_to(mask[s : s + 1], (128, 128)).T

    kv_right_in(0)
    kv_right(1)
    kv_left_in(0)
    kv_left(1)
    arrived(enc_w.at[:, left, core], S_ENC_W)
    to(enc_w.at[0, left, core], S_ENC_W + 2, (c, n, right))
    to(enc_w.at[:, left, core], S_ENC_W + 4, (mate, n, t))
    arrived(enc_w.at[:, right, core], S_ENC_W + 1)
    to(enc_w.at[1, right, core], S_ENC_W + 3, (c, n, left))
    to(enc_w.at[:, right, core], S_ENC_W + 5, (mate, n, t))
    for side, device in enumerate((right, left)):
        arrived(cond_side.at[side], S_COND + side)
        to(cond_side.at[side, 2], (S_COND + 2, S_COND_LAST)[side], (c, n, device), dst=cond_across.at[side])
    kv_right_in(1)
    kv_right(2)
    kv_left_in(1)
    kv_left(2)

    def take(k):
        other = others[k]

        @pl.when(other != n)
        def _():
            arrived(emb.at[k], S_EMB + k)

        @pl.when(other == n)
        def _():
            pltpu.make_async_copy(embed.at[n], emb.at[k], local.at[4]).wait()

        normed[k] = norm_rows(emb[k].astype(jnp.float32), gain_in[...].astype(jnp.float32).reshape(1, 768))

    def encode_heads(shard, states, k):
        query = dot(enc_w[0, shard].reshape(192, 768), normed[k], NT)
        query = query.astype(jnp.bfloat16) * jnp.bfloat16(EHD ** (-0.5))
        rows = []
        for h in range(3):
            at = slice(h * EHD, (h + 1) * EHD)
            both = states[k, at, :]
            scores = dot(both, query[at], TN)[:STRETCH_TOKENS]
            raised = jnp.exp(scores - jnp.max(scores, axis=0, keepdims=True))
            weights = (raised / jnp.sum(raised, axis=0, keepdims=True)).astype(jnp.bfloat16)
            spread = jnp.concatenate([jnp.zeros_like(weights), weights], axis=0)
            rows.append(dot(both, spread, NN).astype(jnp.bfloat16))
        mixed[k, shard] = jnp.concatenate(rows, axis=0)

    def finish(k):
        updated = dot(mixed[k].reshape(768, 128), enc_w[1].reshape(768, 768), TN)
        rows = emb[k].astype(jnp.float32) + updated
        encoded[first + 4 * k] = norm_rows(rows, gain_out[...].astype(jnp.float32).reshape(1, 768))
        to(encoded.at[first + 4 * k], S_AG + 2 * k, (c, n, right))
        to(encoded.at[first + 4 * k], S_AG + 2 * k + 1, (c, n, left))

    take(0)
    encode_heads(t, cond_own, 0)
    arrived(enc_w.at[0, across, core], S_ENC_W + 2)
    to(enc_w.at[0, across, core], S_ENC_W + 6, (mate, n, t))
    arrived(enc_w.at[1, across, core], S_ENC_W + 3)
    to(enc_w.at[1, across, core], S_ENC_W + 7, (mate, n, t))
    out_right_in(0)
    out_right(1)
    out_left_in(0)
    out_left(1)
    arrived(enc_w.at[:, left, 1 - core], S_ENC_W + 4)
    encode_heads(left, cond_side.at[0], 0)
    kv_right_in(2)
    kv_right(3)
    kv_left_in(2)
    arrived(enc_w.at[:, right, 1 - core], S_ENC_W + 5)
    encode_heads(right, cond_side.at[1], 0)
    for side in range(2):
        arrived(cond_across.at[side], (S_COND + 2, S_COND_LAST)[side])
    arrived(enc_w.at[0, across, 1 - core], S_ENC_W + 6)
    encode_heads(across, cond_across, 0)
    arrived(enc_w.at[1, across, 1 - core], S_ENC_W + 7)

    finish(0)
    take(1)
    for shard, states in ((t, cond_own), (left, cond_side.at[0]), (right, cond_side.at[1]), (across, cond_across)):
        encode_heads(shard, states, 1)
    finish(1)

    kv_right_in(3)
    to(kv_w.at[:, :, core], S_KV_MATE, (mate, n, t))
    out_right_in(1)
    out_right(2)
    out_left_in(1)
    out_left(2)
    arrived(kv_w.at[:, :, 1 - core], S_KV_MATE)

    def project(rows):
        made = []
        for i in range(2):
            made.append(dot(rows, kv_w[i].reshape(768, 512), NN).astype(jnp.bfloat16))
        return made

    def project_pair(start):
        rows = jnp.concatenate([encoded[start], encoded[start + 4]], axis=0)
        got_k, got_v = project(rows)
        for k in range(2):
            keys[start + 4 * k] = got_k[k * 128 : (k + 1) * 128]
            values[start + 4 * k] = got_v[k * 128 : (k + 1) * 128]

    def first_of(shard):
        return lax.rem(shard - n + 8, 4)

    project_pair(first)
    def half_of(shard, k, side):
        return encoded.at[first_of(shard) + 4 * k, pl.ds(64 * side, 64)]

    for k in range(2):
        for side, (source, target) in enumerate(((left, right), (right, left))):
            arrived(encoded.at[first_of(source) + 4 * k], S_AG + 2 * k + side)
            to(half_of(source, k, side), S_AG_ON + 2 * k + side, (c, n, target))
    project_pair(first_of(left))
    project_pair(first_of(right))
    out_right_in(2)
    out_right(3)
    out_left_in(2)
    for k in range(2):
        for side in range(2):
            arrived(half_of(across, k, side), S_AG_ON + 2 * k + side)

    project_pair(first_of(across))

    slot_of = []
    for s in range(8):
        place = jnp.int32(0)
        for o in range(1, 8):
            place = jnp.where(slots[o, block] == s, o, place)
        slot_of.append(place)

    lane = lax.broadcasted_iota(jnp.int32, (1, 128), 1)
    use_lane = (lane >= STRETCH_TOKENS - 1) & (lane < 2 * STRETCH_TOKENS - 1)

    def attend(st, h, query_rows):
        at = slice(h * HEAD_WIDTH, (h + 1) * HEAD_WIDTH)
        pair = (slot_of[2 * st], slot_of[2 * st + 1])
        key_rows = jnp.concatenate([keys[p, :, at] for p in pair], axis=0)
        value_rows = jnp.concatenate([values[p, :, at] for p in pair], axis=0)
        allowed = key_mask[2 * st : 2 * st + 2].reshape(256, 128)
        scores = dot(key_rows, query_rows, NT) * HEAD_WIDTH ** (-0.5)
        scores = jnp.where(allowed > 0, scores, -1e30)
        raised = jnp.exp(scores - jnp.max(scores, axis=0, keepdims=True)) * allowed
        sums = jnp.sum(raised, axis=0, keepdims=True)
        use = (sums > 0) & use_lane
        share = jnp.where(use, 1.0 / jnp.where(use, sums, 1.0), 0.0)
        return dot((raised * share).astype(jnp.bfloat16), value_rows, TN)

    heads = [slice(h * HEAD_WIDTH, (h + 1) * HEAD_WIDTH) for h in range(4)]
    arrived(queries_next, S_QUERY)
    fourth = []
    for h, at in enumerate(heads):
        got = attend(3, h, jnp.concatenate([queries[192:256, at], queries_next[:, at]], axis=0))
        rows_send[:, at] = got[64:].astype(jnp.bfloat16)
        fourth.append(got[:64])

    @pl.when(n < 7)
    def _():
        pl.semaphore_wait(ready.at[2], 1)

    to(rows_send, S_PREV, next_device, dst=rows_got)

    def rows_of(shard, start, size):
        return attended.at[shard, pl.ds(start, size)]

    pieces = ((128, 128), (64, 64), (0, 64))

    def leave(i, rows):
        start, size = pieces[i]
        for h, at in enumerate(heads):
            attended[t, start : start + size, at] = rows[h].astype(jnp.bfloat16)
        to(rows_of(t, start, size), S_ATT + 4 * i, (c, n, right))
        to(rows_of(t, start, size), S_ATT + 4 * i + 1, (c, n, left))

    def pass_on(i):
        start, size = pieces[i]
        arrived(rows_of(left, start, size), S_ATT + 4 * i)
        to(rows_of(left, start, size // 2), S_ATT + 4 * i + 2, (c, n, right))
        arrived(rows_of(right, start, size), S_ATT + 4 * i + 1)
        to(rows_of(right, start + size // 2, size // 2), S_ATT + 4 * i + 3, (c, n, left))

    def passed_on(i):
        start, size = pieces[i]
        arrived(rows_of(across, start, size // 2), S_ATT + 4 * i + 2)
        arrived(rows_of(across, start + size // 2, size // 2), S_ATT + 4 * i + 3)

    got = [[attend(st, h, queries[64 * st : 64 * st + 128, at]) for h, at in enumerate(heads)] for st in (2, 1)]
    leave(
        0,
        [
            jnp.concatenate([got[1][h][64:] + got[0][h][:64], got[0][h][64:] + fourth[h]], axis=0)
            for h in range(4)
        ],
    )
    zero = [attend(0, h, queries[0:128, at]) for h, at in enumerate(heads)]
    leave(1, [zero[h][64:] + got[1][h][:64] for h in range(4)])
    arrived(rows_got, S_PREV)
    leave(2, [zero[h][:64] + jnp.where(block > 0, rows_got[:, at].astype(jnp.float32), 0.0) for h, at in enumerate(heads)])
    pass_on(0)
    pass_on(1)

    out_right_in(3)
    for i in range(8):
        at = y if i == 0 else (y - i + 8 if i < 5 else y + i - 4)
        arrived(w_out.at[lax.rem(at, 8), 1 - core], S_OUT_MATE + i)
    own[9].wait()

    def product(shard, rows=slice(0, 256)):
        return dot(attended[shard, rows], w_out[pl.ds(2 * shard, 2)].reshape(512, 1024), NN)

    total[...] = hidden[...].astype(jnp.float32) + product(t)
    pass_on(2)
    total[...] += product(left) + product(right)
    for i, rows in ((0, slice(128, 256)), (1, None), (2, slice(0, 128))):
        passed_on(i)
        if rows is not None:
            output[rows] = (total[rows] + product(across, rows)).astype(jnp.bfloat16)

    for k in range(2):

        @pl.when(first + 4 * k != n)
        def _():
            emb_copy(k).wait_send()

    for made in sent:
        made.wait_send()


def per_device(
    hidden,
    queries,
    key_weight_matrix,
    value_weight_matrix,
    w_out,
    neighbour_embed,
    neighbour_ids,
    neighbour_count,
    slot_seq,
    cond_keys,
    cond_values,
    enc_gain,
    enc_query,
    enc_out,
    final_gain,
):
    vmem, hbm = pl.BlockSpec(memory_space=pltpu.VMEM), pl.BlockSpec(memory_space=pltpu.HBM)
    smem = pl.BlockSpec(memory_space=pltpu.SMEM)
    bf16, f32 = jnp.bfloat16, jnp.float32
    return pl.pallas_call(
        body,
        out_shape=jax.ShapeDtypeStruct((256, 1024), bf16),
        in_specs=[smem, smem, *[hbm] * 11, vmem, vmem],
        out_specs=vmem,
        scratch_shapes=[
            pltpu.VMEM((192, 256), bf16),
            pltpu.VMEM((192, 256), bf16),
            pltpu.VMEM((256, 512), bf16),
            pltpu.VMEM((8, 128), jnp.int32),
            pltpu.VMEM((8, 2, 128, 1024), bf16),
            pltpu.VMEM((256, 1024), bf16),
            pltpu.VMEM((256, 1024), f32),
            pltpu.VMEM((4, 256, 512), bf16),
            pltpu.VMEM((64, 512), bf16),
            pltpu.VMEM((64, 512), bf16),
            pltpu.VMEM((64, 512), bf16),
            pltpu.VMEM((2, 128, 768), bf16),
            pltpu.VMEM((4, 192, 128), bf16),
            pltpu.VMEM((2, 3, 192, 128), bf16),
            pltpu.VMEM((2, 192, 128), bf16),
            pltpu.VMEM((2, 3, 192, 128), bf16),
            pltpu.VMEM((2, 192, 128), bf16),
            pltpu.VMEM((2, 4, 2, 96, 768), bf16),
            pltpu.VMEM((2, 128, 768), bf16),
            pltpu.VMEM((2, 4, 192, 128), bf16),
            pltpu.VMEM((8, 128, 768), bf16),
            pltpu.VMEM((2, 8, 2, 48, 512), bf16),
            pltpu.VMEM((8, 128, 512), bf16),
            pltpu.VMEM((8, 128, 512), bf16),
            pltpu.VMEM((8, 128, 128), f32),
            pltpu.SemaphoreType.DMA((N_SEMS,)),
            pltpu.SemaphoreType.DMA((N_SEMS,)),
            pltpu.SemaphoreType.DMA((11,)),
            pltpu.SemaphoreType.REGULAR((4,)),
        ],
        compiler_params=pltpu.CompilerParams(
            collective_id=0, has_side_effects=True, vmem_limit_bytes=62 * 2**20
        ),
        cost_estimate=pl.CostEstimate(flops=4 * 10**9, bytes_accessed=150 * 10**6, transcendentals=0),
    )(
        slot_seq.T,
        neighbour_count,
        neighbour_embed,
        cond_keys.T,
        cond_values.T,
        enc_query.T.reshape(2, 96, 768),
        enc_out.reshape(2, 96, 768),
        key_weight_matrix,
        value_weight_matrix,
        queries,
        neighbour_ids,
        w_out,
        hidden,
        enc_gain,
        final_gain,
    )


def solution(mesh):
    in_specs = (
        P(("ctx", "nbr"), "tp"),
        P(("ctx", "nbr"), "tp"),
        P("ctx", "tp"),
        P("ctx", "tp"),
        P("ctx", "tp"),
        P(("ctx", "nbr"), None, None),
        P(("ctx", "nbr"), None),
        P(("ctx", "nbr")),
        P(),
        P(("ctx", "nbr"), "tp"),
        P(("ctx", "nbr"), "tp"),
        P(),
        P(None, "tp"),
        P("tp", None),
        P(),
    )
    out_specs = P(("ctx", "nbr"), "tp")
    return jax.shard_map(
        per_device, mesh=mesh, in_specs=in_specs, out_specs=out_specs, check_vma=False
    )
```
